512 devices in a mesh: seq: 64 (over x, z), head: 8 (over y, core).
Axes of the slice: x: 4, y: 4, z: 16, core: 2. Of those that a mesh axis runs over, the one named last changes fastest.
Arguments:
- query_rows: bfloat16 [32768, 2048], P('seq', 'head'), may hold values from -10 to 10
- key_rows: bfloat16 [32768, 2048], P('seq', 'head'), may hold values from -10 to 10
- value_rows: bfloat16 [32768, 2048], P('seq', 'head'), may hold values from -6 to 6
- saved_output: bfloat16 [32768, 2048], P('seq', 'head'), may hold values from -6 to 6
- output_grad: bfloat16 [32768, 2048], P('seq', 'head'), may hold values from -16 to 16
- out_weight: bfloat16 [2048, 2048], P('seq', 'head'), may hold values from -0.125 to 0.125
- cluster_id: int32 [16, 32768], P('head', 'seq'), may hold values from 0 to 63, as said below
- cluster_slot: int32 [16, 32768], P('head', 'seq'), may hold values from 0 to 511, as said below
Outputs:
- query_grad: bfloat16 [32768, 2048], P('seq', 'head')
- key_grad: bfloat16 [32768, 2048], P('seq', 'head')
- value_grad: bfloat16 [32768, 2048], P('seq', 'head')
- weight_grad: float32 [2048, 2048], P('seq', 'head')
The draws below stay inside these ranges and needn't reach their ends.
Inputs may be any that keep to these rules, and one draw needn't show every extreme that they name: `cluster_id`: for every head each of the 64 clusters holds exactly 512 tokens. Index o of seq owns cluster o of every head. In one head, at most 16 of the 512 tokens of one index of seq fall into the clusters owned by one index of seq, and in every head some pairs reach 16. `cluster_slot`: within a head no two tokens share both cluster and slot.
All inputs are finite; a program needn't handle non-finite values.
Results may differ from the reference program's by a relative error of at most 0.008.
Values may be sent and summed in bfloat16 or wider, within the bound.
No kernel may reach another device: no remote copies, remote signals or barrier semaphores. Data moves between devices by JAX's collectives and lax.ppermute only.
A program may use at most 64 MiB of HBM per device.

```python
import math
import jax
import jax.numpy as jnp
from jax import lax

D = 2048
H = 16
DH = 128
CLUSTER = 512
TOK_DEV = 512
TOKENS = 32768
CPD = 1
CAP = 16
N_SEQ = 64


def route_tables(key):
    key = jax.random.fold_in(key, 500)
    owners = N_SEQ
    full = owners // 4
    remain = owners - full
    spread = TOK_DEV - full * CAP
    base_count = spread // remain
    extra = spread - base_count * remain
    moving = 1 if base_count > 0 else 0

    def one_head(head_key):
        keys = jax.random.split(head_key, 5)
        index = jnp.arange(owners, dtype=jnp.int32)
        after = index - full
        level = base_count + (after < extra).astype(jnp.int32)
        moved = jax.random.randint(keys[0], (owners,), 0, max(base_count, 1)) * moving
        partner = jnp.clip(full + 2 * (after // 2), 0, owners - 1)
        shift_amount = moved[partner]
        paired = level + jnp.where(after % 2 == 0, -shift_amount, shift_amount)
        values = jnp.where(after < 0, CAP, paired).astype(jnp.int32)
        counts_base = values[jax.random.permutation(keys[1], owners)]
        labeling = jax.random.permutation(keys[2], owners)
        counts = counts_base[(labeling[None, :] - index[:, None]) % owners]
        cumulative = jnp.cumsum(counts, axis=1)
        start_pair = cumulative - counts
        ranks = jnp.arange(TOK_DEV, dtype=jnp.int32)
        owner_of = jax.vmap(lambda row: jnp.searchsorted(row, ranks, side='right'))(cumulative).astype(jnp.int32)
        within = ranks[None, :] - jnp.take_along_axis(start_pair, owner_of, axis=1)
        offsets = jnp.cumsum(counts, axis=0) - counts
        placed = jnp.take_along_axis(offsets, owner_of, axis=1) + within
        shuffles = jax.vmap(lambda k: jax.random.permutation(k, TOK_DEV))(jax.random.split(keys[3], owners)).astype(jnp.int32)
        spot = shuffles[owner_of, placed]
        cluster = owner_of * CPD + spot // CLUSTER
        slot_value = spot % CLUSTER
        token_order = jax.vmap(lambda k: jax.random.permutation(k, TOK_DEV))(jax.random.split(keys[4], owners)).astype(jnp.int32)
        source_rows = jnp.broadcast_to(index[:, None], (owners, TOK_DEV))
        cluster_tok = jnp.zeros((owners, TOK_DEV), jnp.int32).at[source_rows, token_order].set(cluster)
        slot_tok = jnp.zeros((owners, TOK_DEV), jnp.int32).at[source_rows, token_order].set(slot_value)
        return (cluster_tok.reshape(TOKENS), slot_tok.reshape(TOKENS))
    return jax.vmap(one_head)(jax.random.split(key, H))


def draw_cluster_id(key, part):
    tables = route_tables(key)
    return tables[0]


def draw_cluster_slot(key, part):
    tables = route_tables(key)
    return tables[1]


def draw_query_rows(key, part):
    key = jax.random.fold_in(key, 3)
    rows = jnp.clip(jax.random.normal(key, (TOKENS, H * DH)), -6.0, 6.0)
    return rows.astype(jnp.bfloat16)


def draw_key_rows(key, part):
    key = jax.random.fold_in(key, 4)
    rows = jnp.clip(jax.random.normal(key, (TOKENS, H * DH)), -6.0, 6.0)
    return rows.astype(jnp.bfloat16)


def spiked(values, own_key, source, target, parts, factor):
    owner, partner = [(jnp.arange(values.shape[dim]) // (values.shape[dim] // parts)).reshape([-1 if axis == dim else 1 for axis in range(values.ndim)]) for dim in (source, target)]
    chosen = jax.random.permutation(own_key, parts)[partner]
    strong = (owner == chosen) | (owner == (partner + parts // 2) % parts)
    return jnp.where(strong, factor * values, values)


def block_levels(rng, dims, cuts, low, high):
    gain, own = 1.0, jax.random.fold_in(rng, 6)
    for dim, parts in cuts:
        heights = jnp.exp(jax.random.uniform(jax.random.fold_in(own, dim), (parts,), jnp.float32, low / len(cuts), high / len(cuts)))
        gain = gain * jnp.repeat(heights, dims[dim] // parts).reshape([-1 if axis == dim else 1 for axis in range(len(dims))])
    return gain


def gaussian(stream_key, dims, scale, limit, cuts=(), held_as=jnp.bfloat16):
    loudness = block_levels(stream_key, dims, cuts, -0.22, 0.18) if cuts else 1.0
    drawn = jax.random.normal(stream_key, dims, jnp.float32) * scale * loudness
    return jnp.minimum(jnp.maximum(drawn, -limit), limit).astype(held_as)


def bell_draw_with(stream_key, shape, scale, most, shards, heavy, held_as=jnp.bfloat16):
    values = scale * jax.random.normal(stream_key, shape, jnp.float32)
    if shards:
        values = values * block_levels(stream_key, shape, shards, -0.22, 0.18)
    return jnp.clip(spiked(values, jax.random.fold_in(stream_key, 3), *heavy), -most, most).astype(held_as)


def setup_inputs(seed: int = 0) -> dict:
    seeds = jax.random.split(jax.random.key(seed), 9)
    query_rows = draw_query_rows(jax.random.fold_in(seeds[8], 71), 0)
    key_rows = draw_key_rows(jax.random.fold_in(seeds[8], 71), 0)
    value_rows = gaussian(seeds[2], (TOKENS, H * DH), 1.0, 6.0, ((0, 64), (1, 8)))
    saved_output = gaussian(seeds[3], (TOKENS, H * DH), 1.0, 6.0, ((0, 64), (1, 8)))
    output_grad = bell_draw_with(seeds[4], (TOKENS, D), 1.0, 16.0, ((0, 64), (1, 8)), (0, 1, 64, 4.0))
    out_weight = gaussian(seeds[5], (D, H * DH), D ** -0.5, 0.125, ((0, 64), (1, 8)))
    cluster_id = draw_cluster_id(jax.random.fold_in(seeds[8], 71), 0)
    cluster_slot = draw_cluster_slot(jax.random.fold_in(seeds[8], 71), 0)
    return dict(query_rows=query_rows, key_rows=key_rows, value_rows=value_rows, saved_output=saved_output, output_grad=output_grad, out_weight=out_weight, cluster_id=cluster_id, cluster_slot=cluster_slot)


def attend(queries, key_block, value_block, cotangent, saved, positions):
    score_scale = 1.0 / math.sqrt(DH)
    scores = jnp.einsum('id,jd->ij', queries.astype(jnp.float32), key_block.astype(jnp.float32)) * score_scale
    allowed = positions[None, :] <= positions[:, None]
    scores = jnp.where(allowed, scores, -jnp.inf)
    row_max = lax.optimization_barrier(jnp.max(scores, axis=1, keepdims=True))
    exponent = jnp.exp(scores - row_max)
    softmax_p = exponent / lax.optimization_barrier(jnp.sum(exponent, axis=1, keepdims=True))
    rounded_p = softmax_p.astype(jnp.bfloat16)
    summed = lax.optimization_barrier(jnp.sum(cotangent.astype(jnp.float32) * saved.astype(jnp.float32), axis=1))
    row_term = lax.optimization_barrier(summed.astype(jnp.bfloat16)).astype(jnp.float32)
    grad_prob = jnp.einsum('id,jd->ij', cotangent.astype(jnp.float32), value_block.astype(jnp.float32))
    grad_score = (softmax_p * (grad_prob - row_term[:, None]) * score_scale).astype(jnp.bfloat16)
    grad_query = jnp.einsum('ij,jd->id', grad_score.astype(jnp.float32), key_block.astype(jnp.float32))
    grad_key = jnp.einsum('ij,id->jd', grad_score.astype(jnp.float32), queries.astype(jnp.float32))
    grad_value = jnp.einsum('ij,id->jd', rounded_p.astype(jnp.float32), cotangent.astype(jnp.float32))
    return jnp.concatenate([grad_query, grad_key, grad_value], axis=1).astype(jnp.bfloat16)

def reference(query_rows, key_rows, value_rows, saved_output, output_grad, out_weight, cluster_id, cluster_slot):
    cotangent = jnp.dot(output_grad, out_weight, preferred_element_type=jnp.float32).astype(jnp.bfloat16)
    weight_grad = jnp.dot(output_grad.T, saved_output, preferred_element_type=jnp.float32)
    token_ids = jnp.arange(TOKENS, dtype=jnp.int32)
    clusters = TOKENS // CLUSTER

    def one_head(head_index):
        destination = (cluster_id[head_index] * CLUSTER + cluster_slot[head_index]).astype(jnp.int32)
        members = jnp.zeros((TOKENS,), jnp.int32).at[destination].set(token_ids)

        def columns(source):
            head_block = lax.dynamic_slice_in_dim(source, head_index * DH, DH, 1)
            return head_block[members].reshape(clusters, CLUSTER, DH)
        gathered = (columns(query_rows), columns(key_rows), columns(value_rows), columns(cotangent), columns(saved_output), members.reshape(clusters, CLUSTER))
        result = lax.map(lambda pieces: attend(*pieces), gathered)
        return result.reshape(TOKENS, 3 * DH)[destination]
    gradients = lax.map(one_head, jnp.arange(H, dtype=jnp.int32))
    gradients = gradients.reshape(H, TOKENS, 3, DH).transpose(2, 1, 0, 3).reshape(3, TOKENS, H * DH)
    return (gradients[0], gradients[1], gradients[2], weight_grad)
```

```python
import math

import jax
import jax.numpy as jnp
from jax import lax
from jax.experimental import pallas as pl
from jax.experimental.pallas import tpu as pltpu
from jax.sharding import Mesh
from jax.sharding import PartitionSpec as P

DH = 128
CAP = 16
BLOCK = 256
MASKED = -1e30
SCALE = 1.0 / math.sqrt(DH)
SEQ = ("x", "z")
HEAD = ("y", "core")
PARAMS = pltpu.CompilerParams(vmem_limit_bytes=48 * 1024 * 1024)


def pair_places(ids, owners):
    heads, tokens = ids.shape
    earlier = (
        lax.broadcasted_iota(jnp.int32, (tokens, tokens), 0)
        < lax.broadcasted_iota(jnp.int32, (tokens, tokens), 1)
    ).astype(jnp.float32).astype(jnp.bfloat16)
    owner_iota = lax.broadcasted_iota(jnp.int32, (owners, tokens), 0)
    places = []
    for h in range(heads):
        onehot = jnp.where(owner_iota == ids[h : h + 1, :], 1.0, 0.0)
        before = jnp.dot(onehot.astype(jnp.bfloat16), earlier, preferred_element_type=jnp.float32)
        rank = jnp.sum(onehot * before, axis=0, keepdims=True)
        places.append((onehot, rank))
    return places


def pack_kernel(ids_ref, q_ref, k_ref, v_ref, out_ref):
    owners = out_ref.shape[0]
    ids = ids_ref[...]
    heads, tokens = ids.shape
    slots = owners * CAP
    slot_iota = lax.broadcasted_iota(jnp.int32, (slots, tokens), 0)
    for h, (_, rank) in enumerate(pair_places(ids, owners)):
        place = ids[h : h + 1, :] * CAP + rank.astype(jnp.int32)
        select = jnp.where(slot_iota == place, 1.0, 0.0).astype(jnp.bfloat16)
        for n, ref in enumerate((q_ref, k_ref, v_ref)):
            rows = jnp.dot(
                select, ref[:, h * DH : (h + 1) * DH], preferred_element_type=jnp.float32
            ).astype(jnp.bfloat16)
            out_ref[:, h * CAP : (h + 1) * CAP, n * DH : (n + 1) * DH] = rows.reshape(
                owners, CAP, DH
            )


def cotangent_kernel(ids_ref, grad_ref, weight_ref, saved_ref, out_ref, place_ref):
    owners = out_ref.shape[0]
    ids = ids_ref[...]
    heads, tokens = ids.shape
    slots = owners * CAP
    cot = jnp.dot(grad_ref[...], weight_ref[...], preferred_element_type=jnp.float32).astype(
        jnp.bfloat16
    )
    slot_iota = lax.broadcasted_iota(jnp.int32, (slots, tokens), 0)
    lane = lax.broadcasted_iota(jnp.int32, (tokens, DH), 1)
    row8 = lax.broadcasted_iota(jnp.int32, (8, tokens), 0)
    meta = jnp.zeros((owners, DH), jnp.float32)
    places = pair_places(ids, owners)
    rank_rows = jnp.zeros((8, tokens), jnp.float32)
    place_rows = jnp.zeros((8, tokens), jnp.float32)
    for h, (_, rank) in enumerate(places):
        place = ids[h : h + 1, :].astype(jnp.float32) * CAP + rank
        rank_rows = jnp.where(row8 == h, rank, rank_rows)
        place_rows = jnp.where(row8 == h, place, place_rows)
    rank_columns = rank_rows.T
    place_ref[...] = place_rows.T.astype(jnp.int32)
    for h, (onehot, rank) in enumerate(places):
        g = cot[:, h * DH : (h + 1) * DH]
        o = saved_ref[:, h * DH : (h + 1) * DH]
        row_term = jnp.sum(g.astype(jnp.float32) * o.astype(jnp.float32), axis=1, keepdims=True)
        row_term = row_term.astype(jnp.bfloat16).astype(jnp.float32)
        where_to = rank_columns[:, h : h + 1].astype(jnp.int32) + 2 * CAP * h
        spread = jnp.where(lane == where_to, row_term, 0.0) + jnp.where(
            lane == where_to + CAP, 1.0, 0.0
        )
        meta = meta + jnp.dot(
            onehot.astype(jnp.bfloat16),
            spread.astype(jnp.bfloat16),
            preferred_element_type=jnp.float32,
        )
        place = ids[h : h + 1, :] * CAP + rank.astype(jnp.int32)
        select = jnp.where(slot_iota == place, 1.0, 0.0).astype(jnp.bfloat16)
        rows = jnp.dot(select, g, preferred_element_type=jnp.float32).astype(jnp.bfloat16)
        out_ref[:, h * CAP : (h + 1) * CAP, :] = rows.reshape(owners, CAP, DH)
    meta_lane = lax.broadcasted_iota(jnp.int32, (owners, DH), 1)
    meta = jnp.where((meta_lane & CAP) != 0, (1.0 - meta) * MASKED, meta)
    first = lax.broadcasted_iota(jnp.int32, (owners, 8, DH), 1) == 0
    out_ref[:, heads * CAP :, :] = jnp.where(first, meta[:, None, :], 0.0).astype(jnp.bfloat16)


def attend_kernel(qkv_ref, g_ref, out_ref, prob_ref, score_ref):
    owners = qkv_ref.shape[0]
    heads = qkv_ref.shape[1] // CAP
    slots = owners * CAP
    meta = jnp.sum(g_ref[:, heads * CAP :, :].astype(jnp.float32), axis=1, keepdims=True)
    meta = jnp.broadcast_to(meta, (owners, CAP, DH)).reshape(slots, DH)
    lane = lax.broadcasted_iota(jnp.int32, (slots, DH), 1)
    rank = lax.broadcasted_iota(jnp.int32, (slots, DH), 0) & (CAP - 1)
    later = lax.broadcasted_iota(jnp.int32, (BLOCK, BLOCK), 0) > lax.broadcasted_iota(
        jnp.int32, (BLOCK, BLOCK), 1
    )
    contract_last = (((1,), (1,)), ((), ()))
    contract_first = (((0,), (0,)), ((), ()))

    def rows_of(ref, h, n):
        return ref[:, h * CAP : (h + 1) * CAP, n * DH : (n + 1) * DH].reshape(slots, DH)

    for h in range(heads):
        q, k, v = (rows_of(qkv_ref, h, n) for n in range(3))
        g = rows_of(g_ref, h, 0)
        term_lanes = (lane >= 2 * CAP * h) & (lane < 2 * CAP * h + CAP)
        bias_lanes = (lane >= 2 * CAP * h + CAP) & (lane < 2 * CAP * (h + 1))
        own = jnp.where((lane & (CAP - 1)) == rank, meta, 0.0)
        extra = jnp.where(term_lanes | bias_lanes, own, 0.0).astype(jnp.bfloat16)
        minus_one = jnp.where(term_lanes, -1.0, 0.0).astype(jnp.bfloat16)
        one = jnp.where(bias_lanes, 1.0, 0.0).astype(jnp.bfloat16)
        q_wide = jnp.concatenate([q, one], axis=1)
        k_wide = jnp.concatenate([k, extra], axis=1)
        g_wide = jnp.concatenate([g, extra], axis=1)
        v_wide = jnp.concatenate([v, minus_one], axis=1)
        for start in range(0, slots, BLOCK):
            stop = start + BLOCK
            scores = (
                lax.dot_general(
                    k_wide[:stop], q_wide[start:stop], contract_last,
                    preferred_element_type=jnp.float32,
                )
                * SCALE
            )
            last = jnp.where(later, MASKED, scores[start:stop])
            if start:
                scores = jnp.concatenate([scores[:start], last], axis=0)
            else:
                scores = last
            exponent = jnp.exp(scores - jnp.max(scores, axis=0, keepdims=True))
            prob = exponent * (1.0 / jnp.sum(exponent, axis=0, keepdims=True))
            grad_prob = lax.dot_general(
                v_wide[:stop], g_wide[start:stop], contract_last,
                preferred_element_type=jnp.float32,
            )
            grad_score = (prob * grad_prob * SCALE).astype(jnp.bfloat16)
            prob_ref[:stop, start:stop] = prob.astype(jnp.bfloat16)
            score_ref[:stop, start:stop] = grad_score
            grad_query = lax.dot_general(
                grad_score, k[:stop], contract_first, preferred_element_type=jnp.float32
            )
            out_ref[start // CAP : stop // CAP, h * CAP : (h + 1) * CAP, 0:DH] = (
                grad_query.astype(jnp.bfloat16).reshape(BLOCK // CAP, CAP, DH)
            )
        for start in range(0, slots, BLOCK):
            stop = start + BLOCK
            for n, ref, other in ((1, score_ref, q), (2, prob_ref, g)):
                grad = jnp.dot(
                    ref[start:stop, start:], other[start:], preferred_element_type=jnp.float32
                )
                out_ref[
                    start // CAP : stop // CAP, h * CAP : (h + 1) * CAP, n * DH : (n + 1) * DH
                ] = grad.astype(jnp.bfloat16).reshape(BLOCK // CAP, CAP, DH)


def unpack_kernel(home_ref, place_ref, dq_ref, dk_ref, dv_ref):
    owners = home_ref.shape[0]
    heads = home_ref.shape[1] // CAP
    slots = owners * CAP
    tokens = place_ref.shape[0]
    slot_iota = lax.broadcasted_iota(jnp.int32, (tokens, slots), 1)
    for h in range(heads):
        select = jnp.where(slot_iota == place_ref[:, h : h + 1], 1.0, 0.0).astype(jnp.bfloat16)
        for n, ref in enumerate((dq_ref, dk_ref, dv_ref)):
            rows = home_ref[:, h * CAP : (h + 1) * CAP, n * DH : (n + 1) * DH].reshape(slots, DH)
            ref[:, h * DH : (h + 1) * DH] = jnp.dot(
                select, rows, preferred_element_type=jnp.float32
            ).astype(jnp.bfloat16)


def copies_to_all(block, axis):
    size = lax.axis_size(axis)
    return lax.all_to_all(
        jnp.broadcast_to(block[None], (size, *block.shape)), axis, 0, 0, tiled=True
    )


def local(
    query_rows, key_rows, value_rows, saved_output, output_grad, out_weight, cluster_id, _slot
):
    tokens, width = query_rows.shape
    heads = cluster_id.shape[0]
    owners = lax.axis_size(SEQ)
    bf16 = jnp.bfloat16
    shape = jax.ShapeDtypeStruct

    full_grad = lax.all_gather(output_grad, HEAD, axis=1, tiled=True)
    weight_z = copies_to_all(out_weight, "z").reshape(-1, width)
    weight = copies_to_all(weight_z, "x").reshape(-1, width)

    qkv = pl.pallas_call(
        pack_kernel,
        out_shape=shape((owners, heads * CAP, 3 * DH), bf16),
        compiler_params=PARAMS,
        name="pack_rows",
    )(cluster_id, query_rows, key_rows, value_rows)
    qkv = lax.all_to_all(qkv, SEQ, 0, 0, tiled=True)

    cot, places = pl.pallas_call(
        cotangent_kernel,
        out_shape=(
            shape((owners, heads * CAP + 8, DH), bf16),
            shape((tokens, 8), jnp.int32),
        ),
        compiler_params=PARAMS,
        name="cotangent_rows",
    )(cluster_id, full_grad, weight, saved_output)
    cot = lax.all_to_all(cot, SEQ, 0, 0, tiled=True)

    share = jnp.einsum("tc,td->cd", full_grad, saved_output, preferred_element_type=jnp.float32)
    model = share.shape[0]
    n_x, n_z = lax.axis_size("x"), lax.axis_size("z")
    share = share.astype(bf16).reshape(n_x, model // n_x, width)
    share = lax.all_to_all(share, "x", 0, 0, tiled=True)
    share = jnp.sum(share.astype(jnp.float32), axis=0).astype(bf16)
    share = share.reshape(n_z, model // owners, width)
    share = lax.all_to_all(share, "z", 0, 0, tiled=True)
    weight_grad = jnp.sum(share.astype(jnp.float32), axis=0)

    grads = pl.pallas_call(
        attend_kernel,
        out_shape=shape((owners, heads * CAP, 3 * DH), bf16),
        scratch_shapes=[
            pltpu.VMEM((owners * CAP, owners * CAP), bf16),
            pltpu.VMEM((owners * CAP, owners * CAP), bf16),
        ],
        compiler_params=PARAMS,
        name="attend_cluster",
    )(qkv, cot)
    home = lax.all_to_all(grads, SEQ, 0, 0, tiled=True)
    dq, dk, dv = pl.pallas_call(
        unpack_kernel,
        out_shape=tuple(shape((tokens, width), bf16) for _ in range(3)),
        compiler_params=PARAMS,
        name="unpack_rows",
    )(home, places)
    return dq, dk, dv, weight_grad


def solution(mesh):
    n_seq, n_head = mesh.devices.shape
    n_x, n_y = 4, n_head // 2
    grid = Mesh(mesh.devices.reshape(n_x, n_seq // n_x, n_y, 2), ("x", "z", "y", "core"))
    rows, ids = P(SEQ, HEAD), P(HEAD, SEQ)
    return jax.shard_map(
        local,
        mesh=grid,
        in_specs=(rows,) * 6 + (ids,) * 2,
        out_specs=(rows,) * 4,
        check_vma=False,
    )
```

```python
import math

import jax
import jax.numpy as jnp
from jax import lax
from jax.experimental import pallas as pl
from jax.experimental.pallas import tpu as pltpu
from jax.sharding import Mesh
from jax.sharding import PartitionSpec as P

DH = 128
CAP = 16
BLOCK = 256
MASKED = -1e30
SCALE = 1.0 / math.sqrt(DH)
LOG2_E = math.log2(math.e)
Z = ("z_hi", "z_lo")
SEQ = ("x", *Z)
HEAD = ("y", "core")
PARAMS = pltpu.CompilerParams(vmem_limit_bytes=48 * 1024 * 1024)


def pair_places(ids, owners):
    heads, tokens = ids.shape
    earlier = (
        lax.broadcasted_iota(jnp.int32, (tokens, tokens), 0)
        < lax.broadcasted_iota(jnp.int32, (tokens, tokens), 1)
    ).astype(jnp.float32).astype(jnp.bfloat16)
    owner_iota = lax.broadcasted_iota(jnp.int32, (owners, tokens), 0)
    places = []
    for h in range(heads):
        onehot = jnp.where(owner_iota == ids[h : h + 1, :], 1.0, 0.0)
        before = jnp.dot(onehot.astype(jnp.bfloat16), earlier, preferred_element_type=jnp.float32)
        rank = jnp.sum(onehot * before, axis=0, keepdims=True)
        places.append((onehot, rank))
    return places


def pack_kernel(ids_ref, q_ref, k_ref, v_ref, out_ref):
    owners = out_ref.shape[0]
    ids = ids_ref[...]
    heads, tokens = ids.shape
    slots = owners * CAP
    slot_iota = lax.broadcasted_iota(jnp.int32, (slots, tokens), 0)
    for h, (_, rank) in enumerate(pair_places(ids, owners)):
        place = ids[h : h + 1, :] * CAP + rank.astype(jnp.int32)
        select = jnp.where(slot_iota == place, 1.0, 0.0).astype(jnp.bfloat16)
        for n, ref in enumerate((q_ref, k_ref, v_ref)):
            rows = jnp.dot(
                select, ref[:, h * DH : (h + 1) * DH], preferred_element_type=jnp.float32
            ).astype(jnp.bfloat16)
            out_ref[:, h * CAP : (h + 1) * CAP, n * DH : (n + 1) * DH] = rows.reshape(
                owners, CAP, DH
            )


def cotangent_kernel(ids_ref, grad_ref, weight_ref, saved_ref, out_ref, place_ref):
    owners = out_ref.shape[0]
    ids = ids_ref[...]
    heads, tokens = ids.shape
    slots = owners * CAP
    cot = jnp.dot(grad_ref[...], weight_ref[...], preferred_element_type=jnp.float32).astype(
        jnp.bfloat16
    )
    slot_iota = lax.broadcasted_iota(jnp.int32, (slots, tokens), 0)
    lane = lax.broadcasted_iota(jnp.int32, (tokens, DH), 1)
    row8 = lax.broadcasted_iota(jnp.int32, (8, tokens), 0)
    meta = jnp.zeros((owners, DH), jnp.float32)
    places = pair_places(ids, owners)
    rank_rows = jnp.zeros((8, tokens), jnp.float32)
    place_rows = jnp.zeros((8, tokens), jnp.float32)
    for h, (_, rank) in enumerate(places):
        place = ids[h : h + 1, :].astype(jnp.float32) * CAP + rank
        rank_rows = jnp.where(row8 == h, rank, rank_rows)
        place_rows = jnp.where(row8 == h, place, place_rows)
    rank_columns = rank_rows.T
    place_ref[...] = place_rows.T.astype(jnp.int32)
    for h, (onehot, rank) in enumerate(places):
        g = cot[:, h * DH : (h + 1) * DH]
        o = saved_ref[:, h * DH : (h + 1) * DH]
        row_term = jnp.sum(g.astype(jnp.float32) * o.astype(jnp.float32), axis=1, keepdims=True)
        row_term = row_term.astype(jnp.bfloat16).astype(jnp.float32)
        where_to = rank_columns[:, h : h + 1].astype(jnp.int32) + 2 * CAP * h
        spread = jnp.where(lane == where_to, row_term, 0.0) + jnp.where(
            lane == where_to + CAP, 1.0, 0.0
        )
        meta = meta + jnp.dot(
            onehot.astype(jnp.bfloat16),
            spread.astype(jnp.bfloat16),
            preferred_element_type=jnp.float32,
        )
        place = ids[h : h + 1, :] * CAP + rank.astype(jnp.int32)
        select = jnp.where(slot_iota == place, 1.0, 0.0).astype(jnp.bfloat16)
        rows = jnp.dot(select, g, preferred_element_type=jnp.float32).astype(jnp.bfloat16)
        out_ref[:, h * CAP : (h + 1) * CAP, :] = rows.reshape(owners, CAP, DH)
    meta_lane = lax.broadcasted_iota(jnp.int32, (owners, DH), 1)
    meta = jnp.where((meta_lane & CAP) != 0, (1.0 - meta) * MASKED, meta)
    first = lax.broadcasted_iota(jnp.int32, (owners, 8, DH), 1) == 0
    out_ref[:, heads * CAP :, :] = jnp.where(first, meta[:, None, :], 0.0).astype(jnp.bfloat16)


def attend_kernel(qkv_ref, g_ref, out_ref, prob_ref, score_ref):
    owners = qkv_ref.shape[0]
    heads = qkv_ref.shape[1] // CAP
    slots = owners * CAP
    meta = jnp.sum(g_ref[:, heads * CAP :, :].astype(jnp.float32), axis=1, keepdims=True)
    meta = jnp.broadcast_to(meta, (owners, CAP, DH)).reshape(slots, DH)
    lane = lax.broadcasted_iota(jnp.int32, (slots, DH), 1)
    rank = lax.broadcasted_iota(jnp.int32, (slots, DH), 0) & (CAP - 1)
    later = lax.broadcasted_iota(jnp.int32, (BLOCK, BLOCK), 0) > lax.broadcasted_iota(
        jnp.int32, (BLOCK, BLOCK), 1
    )
    contract_last = (((1,), (1,)), ((), ()))
    contract_first = (((0,), (0,)), ((), ()))

    def rows_of(ref, h, n):
        return ref[:, h * CAP : (h + 1) * CAP, n * DH : (n + 1) * DH].reshape(slots, DH)

    for h in range(heads):
        q, k, v = (rows_of(qkv_ref, h, n) for n in range(3))
        g = rows_of(g_ref, h, 0)
        term_lanes = (lane >= 2 * CAP * h) & (lane < 2 * CAP * h + CAP)
        bias_lanes = (lane >= 2 * CAP * h + CAP) & (lane < 2 * CAP * (h + 1))
        own = jnp.where((lane & (CAP - 1)) == rank, meta, 0.0)
        extra = jnp.where(term_lanes | bias_lanes, own, 0.0).astype(jnp.bfloat16)
        minus_one = jnp.where(term_lanes, -1.0, 0.0).astype(jnp.bfloat16)
        one = jnp.where(bias_lanes, 1.0, 0.0).astype(jnp.bfloat16)
        q_wide = jnp.concatenate([q, one], axis=1)
        k_wide = jnp.concatenate([k, extra], axis=1)
        g_wide = jnp.concatenate([g, extra], axis=1)
        v_wide = jnp.concatenate([v, minus_one], axis=1)
        for start in range(0, slots, BLOCK):
            stop = start + BLOCK
            scores = lax.dot_general(
                k_wide[:stop], q_wide[start:stop], contract_last,
                preferred_element_type=jnp.float32,
            )
            last = jnp.where(later, MASKED, scores[start:stop])
            if start:
                scores = jnp.concatenate([scores[:start], last], axis=0)
            else:
                scores = last
            row_max = jnp.max(scores, axis=0, keepdims=True)
            exponent = jnp.exp2((scores - row_max) * (SCALE * LOG2_E))
            inverse = 1.0 / jnp.sum(exponent, axis=0, keepdims=True)
            grad_prob = lax.dot_general(
                v_wide[:stop], g_wide[start:stop], contract_last,
                preferred_element_type=jnp.float32,
            )
            grad_score = (exponent * (inverse * SCALE) * grad_prob).astype(jnp.bfloat16)
            prob_ref[:stop, start:stop] = (exponent * inverse).astype(jnp.bfloat16)
            score_ref[:stop, start:stop] = grad_score
            grad_query = lax.dot_general(
                grad_score, k[:stop], contract_first, preferred_element_type=jnp.float32
            )
            out_ref[start // CAP : stop // CAP, h * CAP : (h + 1) * CAP, 0:DH] = (
                grad_query.astype(jnp.bfloat16).reshape(BLOCK // CAP, CAP, DH)
            )
        for start in range(0, slots, BLOCK):
            stop = start + BLOCK
            for n, ref, other in ((1, score_ref, q), (2, prob_ref, g)):
                grad = jnp.dot(
                    ref[start:stop, start:], other[start:], preferred_element_type=jnp.float32
                )
                out_ref[
                    start // CAP : stop // CAP, h * CAP : (h + 1) * CAP, n * DH : (n + 1) * DH
                ] = grad.astype(jnp.bfloat16).reshape(BLOCK // CAP, CAP, DH)


def unpack_kernel(home_ref, place_ref, dq_ref, dk_ref, dv_ref):
    owners = home_ref.shape[0]
    heads = home_ref.shape[1] // CAP
    slots = owners * CAP
    tokens = place_ref.shape[0]
    slot_iota = lax.broadcasted_iota(jnp.int32, (tokens, slots), 1)
    for h in range(heads):
        select = jnp.where(slot_iota == place_ref[:, h : h + 1], 1.0, 0.0).astype(jnp.bfloat16)
        for n, ref in enumerate((dq_ref, dk_ref, dv_ref)):
            rows = home_ref[:, h * CAP : (h + 1) * CAP, n * DH : (n + 1) * DH].reshape(slots, DH)
            ref[:, h * DH : (h + 1) * DH] = jnp.dot(
                select, rows, preferred_element_type=jnp.float32
            ).astype(jnp.bfloat16)


def copies_to_all(block, axis):
    size = lax.axis_size(axis)
    return lax.all_to_all(
        jnp.broadcast_to(block[None], (size, *block.shape)), axis, 0, 0, tiled=True
    )


def after(value, earlier):
    return lax.optimization_barrier((value, earlier))[0]


def local(
    query_rows, key_rows, value_rows, saved_output, output_grad, out_weight, cluster_id, _slot
):
    tokens, width = query_rows.shape
    heads = cluster_id.shape[0]
    owners = lax.axis_size(SEQ)
    bf16 = jnp.bfloat16
    shape = jax.ShapeDtypeStruct

    full_grad = lax.all_gather(output_grad, HEAD, axis=1, tiled=True)
    weight_z = copies_to_all(out_weight, Z).reshape(-1, width)
    weight = lax.all_gather(weight_z, "x", axis=0, tiled=True)

    qkv = pl.pallas_call(
        pack_kernel,
        out_shape=shape((owners, heads * CAP, 3 * DH), bf16),
        compiler_params=PARAMS,
        name="pack_rows",
    )(cluster_id, query_rows, key_rows, value_rows)
    qkv = lax.all_to_all(after(qkv, weight_z), SEQ, 0, 0, tiled=True)

    cot, places = pl.pallas_call(
        cotangent_kernel,
        out_shape=(
            shape((owners, heads * CAP + 8, DH), bf16),
            shape((tokens, 8), jnp.int32),
        ),
        compiler_params=PARAMS,
        name="cotangent_rows",
    )(cluster_id, full_grad, weight, saved_output)
    share = jnp.einsum("tc,td->cd", full_grad, saved_output, preferred_element_type=jnp.float32)
    n_x, n_hi, n_lo = (lax.axis_size(axis) for axis in SEQ)
    share = share.reshape(n_x, n_hi, n_lo, -1, width).transpose(0, 2, 1, 3, 4)
    share = after(share.reshape(full_grad.shape[1], width), weight)
    cot = lax.all_to_all(after(cot, (share, qkv)), SEQ, 0, 0, tiled=True)
    share = lax.psum_scatter(share, "x", scatter_dimension=0, tiled=True)
    share = lax.psum_scatter(share, "z_lo", scatter_dimension=0, tiled=True)

    grads = pl.pallas_call(
        attend_kernel,
        out_shape=shape((owners, heads * CAP, 3 * DH), bf16),
        scratch_shapes=[
            pltpu.VMEM((owners * CAP, owners * CAP), bf16),
            pltpu.VMEM((owners * CAP, owners * CAP), bf16),
        ],
        compiler_params=PARAMS,
        name="attend_cluster",
    )(qkv, cot)
    home = lax.all_to_all(after(grads, share), SEQ, 0, 0, tiled=True)
    weight_grad = lax.psum_scatter(share, "z_hi", scatter_dimension=0, tiled=True)
    dq, dk, dv = pl.pallas_call(
        unpack_kernel,
        out_shape=tuple(shape((tokens, width), bf16) for _ in range(3)),
        compiler_params=PARAMS,
        name="unpack_rows",
    )(home, places)
    return dq, dk, dv, weight_grad


def solution(mesh):
    n_head = mesh.devices.shape[1]
    grid = Mesh(mesh.devices.reshape(4, 4, 4, n_head // 2, 2), (*SEQ, *HEAD))
    rows, ids = P(SEQ, HEAD), P(HEAD, SEQ)
    return jax.shard_map(
        local,
        mesh=grid,
        in_specs=(rows,) * 6 + (ids,) * 2,
        out_specs=(rows,) * 4,
        check_vma=False,
    )
```

```python
import math

import jax
import jax.numpy as jnp
from jax import lax
from jax.experimental import pallas as pl
from jax.experimental.pallas import tpu as pltpu
from jax.sharding import Mesh
from jax.sharding import PartitionSpec as P

DH = 128
CAP = 16
BLOCK = 256
MASKED = -1e30
SCALE = 1.0 / math.sqrt(DH)
LOG2_E = math.log2(math.e)
Z = ("z_hi", "z_lo")
SEQ = ("x", *Z)
HEAD = ("y", "core")
EARLY = pl.CostEstimate(flops=70_000_000_000, bytes_accessed=0, transcendentals=0)
PARAMS = pltpu.CompilerParams(vmem_limit_bytes=24 * 1024 * 1024)


def pair_places(ids, owners):
    heads, tokens = ids.shape
    earlier = (
        lax.broadcasted_iota(jnp.int32, (tokens, tokens), 0)
        < lax.broadcasted_iota(jnp.int32, (tokens, tokens), 1)
    ).astype(jnp.float32).astype(jnp.bfloat16)
    owner_iota = lax.broadcasted_iota(jnp.int32, (owners, tokens), 0)
    places = []
    for h in range(heads):
        onehot = jnp.where(owner_iota == ids[h : h + 1, :], 1.0, 0.0)
        before = jnp.dot(onehot.astype(jnp.bfloat16), earlier, preferred_element_type=jnp.float32)
        rank = jnp.sum(onehot * before, axis=0, keepdims=True)
        places.append((onehot, rank))
    return places


def pack_kernel(ids_ref, q_ref, k_ref, v_ref, out_ref):
    owners = out_ref.shape[0]
    ids = ids_ref[...]
    heads, tokens = ids.shape
    slots = owners * CAP
    slot_iota = lax.broadcasted_iota(jnp.int32, (slots, tokens), 0)
    for h, (_, rank) in enumerate(pair_places(ids, owners)):
        place = ids[h : h + 1, :] * CAP + rank.astype(jnp.int32)
        select = jnp.where(slot_iota == place, 1.0, 0.0).astype(jnp.bfloat16)
        for n, ref in enumerate((q_ref, k_ref, v_ref)):
            rows = jnp.dot(
                select, ref[:, h * DH : (h + 1) * DH], preferred_element_type=jnp.float32
            ).astype(jnp.bfloat16)
            out_ref[:, h * CAP : (h + 1) * CAP, n * DH : (n + 1) * DH] = rows.reshape(
                owners, CAP, DH
            )


def cotangent_kernel(ids_ref, grad_ref, weight_ref, saved_ref, out_ref, place_ref):
    owners = out_ref.shape[0]
    ids = ids_ref[...]
    heads, tokens = ids.shape
    slots = owners * CAP
    cot = jnp.dot(grad_ref[...], weight_ref[...], preferred_element_type=jnp.float32).astype(
        jnp.bfloat16
    )
    slot_iota = lax.broadcasted_iota(jnp.int32, (slots, tokens), 0)
    lane = lax.broadcasted_iota(jnp.int32, (tokens, DH), 1)
    row8 = lax.broadcasted_iota(jnp.int32, (8, tokens), 0)
    meta = jnp.zeros((owners, DH), jnp.float32)
    places = pair_places(ids, owners)
    rank_rows = jnp.zeros((8, tokens), jnp.float32)
    place_rows = jnp.zeros((8, tokens), jnp.float32)
    for h, (_, rank) in enumerate(places):
        place = ids[h : h + 1, :].astype(jnp.float32) * CAP + rank
        rank_rows = jnp.where(row8 == h, rank, rank_rows)
        place_rows = jnp.where(row8 == h, place, place_rows)
    rank_columns = rank_rows.T
    place_ref[...] = place_rows.T.astype(jnp.int32)
    for h, (onehot, rank) in enumerate(places):
        g = cot[:, h * DH : (h + 1) * DH]
        o = saved_ref[:, h * DH : (h + 1) * DH]
        row_term = jnp.sum(g.astype(jnp.float32) * o.astype(jnp.float32), axis=1, keepdims=True)
        row_term = row_term.astype(jnp.bfloat16).astype(jnp.float32)
        where_to = rank_columns[:, h : h + 1].astype(jnp.int32) + 2 * CAP * h
        spread = jnp.where(lane == where_to, row_term, 0.0) + jnp.where(
            lane == where_to + CAP, 1.0, 0.0
        )
        meta = meta + jnp.dot(
            onehot.astype(jnp.bfloat16),
            spread.astype(jnp.bfloat16),
            preferred_element_type=jnp.float32,
        )
        place = ids[h : h + 1, :] * CAP + rank.astype(jnp.int32)
        select = jnp.where(slot_iota == place, 1.0, 0.0).astype(jnp.bfloat16)
        rows = jnp.dot(select, g, preferred_element_type=jnp.float32).astype(jnp.bfloat16)
        out_ref[:, h * CAP : (h + 1) * CAP, :] = rows.reshape(owners, CAP, DH)
    meta_lane = lax.broadcasted_iota(jnp.int32, (owners, DH), 1)
    meta = jnp.where((meta_lane & CAP) != 0, (1.0 - meta) * MASKED, meta)
    first = lax.broadcasted_iota(jnp.int32, (owners, 8, DH), 1) == 0
    out_ref[:, heads * CAP :, :] = jnp.where(first, meta[:, None, :], 0.0).astype(jnp.bfloat16)


def attend_kernel(qkv_ref, g_ref, out_ref, prob_ref, score_ref):
    owners = qkv_ref.shape[0]
    heads = qkv_ref.shape[1] // CAP
    slots = owners * CAP
    meta = jnp.sum(g_ref[:, heads * CAP :, :].astype(jnp.float32), axis=1, keepdims=True)
    meta = jnp.broadcast_to(meta, (owners, CAP, DH)).reshape(slots, DH)
    lane = lax.broadcasted_iota(jnp.int32, (slots, DH), 1)
    rank = lax.broadcasted_iota(jnp.int32, (slots, DH), 0) & (CAP - 1)
    later = lax.broadcasted_iota(jnp.int32, (BLOCK, BLOCK), 0) > lax.broadcasted_iota(
        jnp.int32, (BLOCK, BLOCK), 1
    )
    contract_last = (((1,), (1,)), ((), ()))
    contract_first = (((0,), (0,)), ((), ()))

    def rows_of(ref, h, n):
        return ref[:, h * CAP : (h + 1) * CAP, n * DH : (n + 1) * DH].reshape(slots, DH)

    for h in range(heads):
        q, k, v = (rows_of(qkv_ref, h, n) for n in range(3))
        g = rows_of(g_ref, h, 0)
        term_lanes = (lane >= 2 * CAP * h) & (lane < 2 * CAP * h + CAP)
        bias_lanes = (lane >= 2 * CAP * h + CAP) & (lane < 2 * CAP * (h + 1))
        own = jnp.where((lane & (CAP - 1)) == rank, meta, 0.0)
        extra = jnp.where(term_lanes | bias_lanes, own, 0.0).astype(jnp.bfloat16)
        minus_one = jnp.where(term_lanes, -1.0, 0.0).astype(jnp.bfloat16)
        one = jnp.where(bias_lanes, 1.0, 0.0).astype(jnp.bfloat16)
        k_turned = k.T
        q_wide = jnp.concatenate([q, one], axis=1)
        k_wide = jnp.concatenate([k, extra], axis=1)
        g_wide = jnp.concatenate([g, extra], axis=1)
        v_wide = jnp.concatenate([v, minus_one], axis=1)
        for start in range(0, slots, BLOCK):
            stop = start + BLOCK
            scores = lax.dot_general(
                k_wide[:stop], q_wide[start:stop], contract_last,
                preferred_element_type=jnp.float32,
            )
            last = jnp.where(later, MASKED, scores[start:stop])
            if start:
                scores = jnp.concatenate([scores[:start], last], axis=0)
            else:
                scores = last
            row_max = jnp.max(scores, axis=0, keepdims=True)
            exponent = jnp.exp2((scores - row_max) * (SCALE * LOG2_E))
            inverse = 1.0 / jnp.sum(exponent, axis=0, keepdims=True)
            grad_prob = lax.dot_general(
                v_wide[:stop], g_wide[start:stop], contract_last,
                preferred_element_type=jnp.float32,
            )
            grad_score = (exponent * (inverse * SCALE) * grad_prob).astype(jnp.bfloat16)
            prob_ref[:stop, start:stop] = (exponent * inverse).astype(jnp.bfloat16)
            score_ref[:stop, start:stop] = grad_score
        for start in range(0, slots, BLOCK):
            stop = start + BLOCK
            grad_query = jnp.dot(
                k_turned[:, :stop], score_ref[:stop, start:stop], preferred_element_type=jnp.float32
            ).T
            out_ref[start // CAP : stop // CAP, h * CAP : (h + 1) * CAP, 0:DH] = (
                grad_query.astype(jnp.bfloat16).reshape(BLOCK // CAP, CAP, DH)
            )
            for n, ref, other in ((1, score_ref, q), (2, prob_ref, g)):
                grad = jnp.dot(
                    ref[start:stop, start:], other[start:], preferred_element_type=jnp.float32
                )
                out_ref[
                    start // CAP : stop // CAP, h * CAP : (h + 1) * CAP, n * DH : (n + 1) * DH
                ] = grad.astype(jnp.bfloat16).reshape(BLOCK // CAP, CAP, DH)


def copy_kernel(from_ref, to_ref):
    to_ref[...] = from_ref[...]


def unpack_kernel(home_ref, place_ref, dq_ref, dk_ref, dv_ref):
    owners = home_ref.shape[0]
    heads = home_ref.shape[1] // CAP
    slots = owners * CAP
    tokens = place_ref.shape[0]
    slot_iota = lax.broadcasted_iota(jnp.int32, (tokens, slots), 1)
    for h in range(heads):
        select = jnp.where(slot_iota == place_ref[:, h : h + 1], 1.0, 0.0).astype(jnp.bfloat16)
        for n, ref in enumerate((dq_ref, dk_ref, dv_ref)):
            rows = home_ref[:, h * CAP : (h + 1) * CAP, n * DH : (n + 1) * DH].reshape(slots, DH)
            ref[:, h * DH : (h + 1) * DH] = jnp.dot(
                select, rows, preferred_element_type=jnp.float32
            ).astype(jnp.bfloat16)


def copies_to_all(block, axis):
    size = lax.axis_size(axis)
    return lax.all_to_all(
        jnp.broadcast_to(block[None], (size, *block.shape)), axis, 0, 0, tiled=True
    )


def after(value, earlier):
    return lax.optimization_barrier((value, earlier))[0]


def local(
    query_rows, key_rows, value_rows, saved_output, output_grad, out_weight, cluster_id, _slot
):
    tokens, width = query_rows.shape
    heads = cluster_id.shape[0]
    owners = lax.axis_size(SEQ)
    bf16 = jnp.bfloat16
    shape = jax.ShapeDtypeStruct

    full_grad = lax.all_gather(output_grad, HEAD, axis=1, tiled=True)
    weight_z = copies_to_all(out_weight, Z).reshape(-1, width)
    weight = lax.all_gather(weight_z, "x", axis=0, tiled=True)

    qkv = pl.pallas_call(
        pack_kernel,
        out_shape=shape((owners, heads * CAP, 3 * DH), bf16),
        compiler_params=PARAMS,
        name="pack_rows",
    )(cluster_id, query_rows, key_rows, value_rows)
    qkv = lax.all_to_all(after(qkv, weight_z), SEQ, 0, 0, tiled=True)

    cot, places = pl.pallas_call(
        cotangent_kernel,
        out_shape=(
            shape((owners, heads * CAP + 8, DH), bf16),
            shape((tokens, 8), jnp.int32),
        ),
        compiler_params=PARAMS,
        name="cotangent_rows",
    )(cluster_id, full_grad, weight, saved_output)
    share = jnp.einsum("tc,td->cd", full_grad, saved_output, preferred_element_type=jnp.float32)
    share = after(share, weight)
    cot = lax.all_to_all(after(cot, (share, qkv)), SEQ, 0, 0, tiled=True)
    share = lax.psum_scatter(share, "x", scatter_dimension=0, tiled=True)
    weight_grad = pl.pallas_call(
        copy_kernel,
        out_shape=shape(out_weight.shape, jnp.float32),
        compiler_params=PARAMS,
        cost_estimate=EARLY,
        name="weight_grad",
    )(lax.psum_scatter(share, Z, scatter_dimension=0, tiled=True))

    grads = pl.pallas_call(
        attend_kernel,
        out_shape=shape((owners, heads * CAP, 3 * DH), bf16),
        scratch_shapes=[
            pltpu.VMEM((owners * CAP, owners * CAP), bf16),
            pltpu.VMEM((owners * CAP, owners * CAP), bf16),
        ],
        compiler_params=PARAMS,
        name="attend_cluster",
    )(qkv, cot)
    home = lax.all_to_all(grads, SEQ, 0, 0, tiled=True)
    dq, dk, dv = pl.pallas_call(
        unpack_kernel,
        out_shape=tuple(shape((tokens, width), bf16) for _ in range(3)),
        compiler_params=PARAMS,
        name="unpack_rows",
    )(home, places)
    return dq, dk, dv, weight_grad


def solution(mesh):
    n_head = mesh.devices.shape[1]
    grid = Mesh(mesh.devices.reshape(4, 4, 4, n_head // 2, 2), (*SEQ, *HEAD))
    rows, ids = P(SEQ, HEAD), P(HEAD, SEQ)
    return jax.shard_map(
        local,
        mesh=grid,
        in_specs=(rows,) * 6 + (ids,) * 2,
        out_specs=(rows,) * 4,
        check_vma=False,
    )
```

```python
import math

import jax
import jax.numpy as jnp
from jax import lax
from jax.experimental import pallas as pl
from jax.experimental.pallas import tpu as pltpu
from jax.sharding import Mesh
from jax.sharding import PartitionSpec as P

DH = 128
CAP = 16
PAIR = 2 * CAP + 2
BLOCK = 256
MASKED = -1e30
SCALE = 1.0 / math.sqrt(DH)
LOG2_E = math.log2(math.e)
Z = ("z_hi", "z_lo")
SEQ = ("x", *Z)
HEAD = ("y", "core")
EARLY = pl.CostEstimate(flops=70_000_000_000, bytes_accessed=0, transcendentals=0)
PARAMS = pltpu.CompilerParams(vmem_limit_bytes=24 * 1024 * 1024)


def pair_places(ids, owners):
    heads, tokens = ids.shape
    earlier = (
        lax.broadcasted_iota(jnp.int32, (tokens, tokens), 0)
        < lax.broadcasted_iota(jnp.int32, (tokens, tokens), 1)
    ).astype(jnp.float32).astype(jnp.bfloat16)
    owner_iota = lax.broadcasted_iota(jnp.int32, (owners, tokens), 0)
    places = []
    for h in range(heads):
        onehot = jnp.where(owner_iota == ids[h : h + 1, :], 1.0, 0.0)
        before = jnp.dot(onehot.astype(jnp.bfloat16), earlier, preferred_element_type=jnp.float32)
        rank = jnp.sum(onehot * before, axis=0, keepdims=True)
        places.append((onehot, rank))
    return places


def pack_kernel(ids_ref, q_ref, k_ref, v_ref, out_ref):
    owners = out_ref.shape[0]
    ids = ids_ref[...]
    heads, tokens = ids.shape
    slots = owners * CAP
    slot_iota = lax.broadcasted_iota(jnp.int32, (slots, tokens), 0)
    for h, (_, rank) in enumerate(pair_places(ids, owners)):
        place = ids[h : h + 1, :] * CAP + rank.astype(jnp.int32)
        select = jnp.where(slot_iota == place, 1.0, 0.0).astype(jnp.bfloat16)
        for n, ref in enumerate((q_ref, k_ref, v_ref)):
            rows = jnp.dot(
                select, ref[:, h * DH : (h + 1) * DH], preferred_element_type=jnp.float32
            ).astype(jnp.bfloat16)
            out_ref[:, h * CAP : (h + 1) * CAP, n * DH : (n + 1) * DH] = rows.reshape(
                owners, CAP, DH
            )


def cotangent_kernel(ids_ref, grad_ref, weight_ref, saved_ref, out_ref, place_ref):
    sent = out_ref.shape[0]
    owners = sent // PAIR
    ids = ids_ref[...]
    heads, tokens = ids.shape
    cot = jnp.dot(grad_ref[...], weight_ref[...], preferred_element_type=jnp.float32).astype(
        jnp.bfloat16
    )
    row_iota = lax.broadcasted_iota(jnp.int32, (sent, tokens), 0)
    lane = lax.broadcasted_iota(jnp.int32, (tokens, DH), 1)
    row8 = lax.broadcasted_iota(jnp.int32, (8, tokens), 0)
    meta = jnp.zeros((owners, DH), jnp.float32)
    message = jnp.zeros((sent, DH), jnp.float32)
    places = pair_places(ids, owners)
    rank_rows = jnp.zeros((8, tokens), jnp.float32)
    place_rows = jnp.zeros((8, tokens), jnp.float32)
    for h, (_, rank) in enumerate(places):
        place = ids[h : h + 1, :].astype(jnp.float32) * CAP + rank
        rank_rows = jnp.where(row8 == h, rank, rank_rows)
        place_rows = jnp.where(row8 == h, place, place_rows)
    rank_columns = rank_rows.T
    place_ref[...] = place_rows.T.astype(jnp.int32)
    for h, (onehot, rank) in enumerate(places):
        g = cot[:, h * DH : (h + 1) * DH]
        o = saved_ref[:, h * DH : (h + 1) * DH]
        row_term = jnp.sum(g.astype(jnp.float32) * o.astype(jnp.float32), axis=1, keepdims=True)
        row_term = row_term.astype(jnp.bfloat16).astype(jnp.float32)
        where_to = rank_columns[:, h : h + 1].astype(jnp.int32) + 2 * CAP * h
        spread = jnp.where(lane == where_to, row_term, 0.0) + jnp.where(
            lane == where_to + CAP, 1.0, 0.0
        )
        meta = meta + jnp.dot(
            onehot.astype(jnp.bfloat16),
            spread.astype(jnp.bfloat16),
            preferred_element_type=jnp.float32,
        )
        place = ids[h : h + 1, :] * PAIR + h * CAP + rank.astype(jnp.int32)
        select = jnp.where(row_iota == place, 1.0, 0.0).astype(jnp.bfloat16)
        message = message + jnp.dot(select, g, preferred_element_type=jnp.float32)
    meta_lane = lax.broadcasted_iota(jnp.int32, (owners, DH), 1)
    meta = jnp.where((meta_lane & CAP) != 0, (1.0 - meta) * MASKED, meta)
    meta_row = lax.broadcasted_iota(jnp.int32, (sent, owners), 1) * PAIR + heads * CAP
    select = lax.broadcasted_iota(jnp.int32, (sent, owners), 0) == meta_row
    message = message + jnp.dot(
        jnp.where(select, 1.0, 0.0).astype(jnp.bfloat16),
        meta.astype(jnp.bfloat16),
        preferred_element_type=jnp.float32,
    )
    out_ref[...] = message.astype(jnp.bfloat16)


def attend_kernel(qkv_ref, g_ref, out_ref, prob_ref, score_ref):
    owners = qkv_ref.shape[0]
    heads = qkv_ref.shape[1] // CAP
    slots = owners * CAP
    meta = jnp.concatenate(
        [
            jnp.broadcast_to(
                g_ref[first : first + 2, :].astype(jnp.float32)[:1], (CAP, DH)
            )
            for first in range(heads * CAP, owners * PAIR, PAIR)
        ],
        axis=0,
    )
    lane = lax.broadcasted_iota(jnp.int32, (slots, DH), 1)
    rank = lax.broadcasted_iota(jnp.int32, (slots, DH), 0) & (CAP - 1)
    later = lax.broadcasted_iota(jnp.int32, (BLOCK, BLOCK), 0) > lax.broadcasted_iota(
        jnp.int32, (BLOCK, BLOCK), 1
    )
    contract_last = (((1,), (1,)), ((), ()))
    contract_first = (((0,), (0,)), ((), ()))

    def rows_of(h, n):
        return qkv_ref[:, h * CAP : (h + 1) * CAP, n * DH : (n + 1) * DH].reshape(slots, DH)

    for h in range(heads):
        q, k, v = (rows_of(h, n) for n in range(3))
        g = jnp.concatenate(
            [g_ref[n : n + CAP, :] for n in range(h * CAP, owners * PAIR, PAIR)], axis=0
        )
        term_lanes = (lane >= 2 * CAP * h) & (lane < 2 * CAP * h + CAP)
        bias_lanes = (lane >= 2 * CAP * h + CAP) & (lane < 2 * CAP * (h + 1))
        own = jnp.where((lane & (CAP - 1)) == rank, meta, 0.0)
        extra = jnp.where(term_lanes | bias_lanes, own, 0.0).astype(jnp.bfloat16)
        minus_one = jnp.where(term_lanes, -1.0, 0.0).astype(jnp.bfloat16)
        one = jnp.where(bias_lanes, 1.0, 0.0).astype(jnp.bfloat16)
        k_turned = k.T
        q_wide = jnp.concatenate([q, one], axis=1)
        k_wide = jnp.concatenate([k, extra], axis=1)
        g_wide = jnp.concatenate([g, extra], axis=1)
        v_wide = jnp.concatenate([v, minus_one], axis=1)
        for start in range(0, slots, BLOCK):
            stop = start + BLOCK
            scores = lax.dot_general(
                k_wide[:stop], q_wide[start:stop], contract_last,
                preferred_element_type=jnp.float32,
            )
            last = jnp.where(later, MASKED, scores[start:stop])
            if start:
                scores = jnp.concatenate([scores[:start], last], axis=0)
            else:
                scores = last
            row_max = jnp.max(scores, axis=0, keepdims=True)
            exponent = jnp.exp2((scores - row_max) * (SCALE * LOG2_E))
            inverse = 1.0 / jnp.sum(exponent, axis=0, keepdims=True)
            grad_prob = lax.dot_general(
                v_wide[:stop], g_wide[start:stop], contract_last,
                preferred_element_type=jnp.float32,
            )
            grad_score = (exponent * (inverse * SCALE) * grad_prob).astype(jnp.bfloat16)
            prob_ref[:stop, start:stop] = (exponent * inverse).astype(jnp.bfloat16)
            score_ref[:stop, start:stop] = grad_score
        for start in range(0, slots, BLOCK):
            stop = start + BLOCK
            grad_query = jnp.dot(
                k_turned[:, :stop], score_ref[:stop, start:stop], preferred_element_type=jnp.float32
            ).T
            out_ref[start // CAP : stop // CAP, h * CAP : (h + 1) * CAP, 0:DH] = (
                grad_query.astype(jnp.bfloat16).reshape(BLOCK // CAP, CAP, DH)
            )
            for n, ref, other in ((1, score_ref, q), (2, prob_ref, g)):
                grad = jnp.dot(
                    ref[start:stop, start:], other[start:], preferred_element_type=jnp.float32
                )
                out_ref[
                    start // CAP : stop // CAP, h * CAP : (h + 1) * CAP, n * DH : (n + 1) * DH
                ] = grad.astype(jnp.bfloat16).reshape(BLOCK // CAP, CAP, DH)


def copy_kernel(from_ref, to_ref):
    to_ref[...] = from_ref[...]


def unpack_kernel(home_ref, place_ref, dq_ref, dk_ref, dv_ref):
    owners = home_ref.shape[0]
    heads = home_ref.shape[1] // CAP
    slots = owners * CAP
    tokens = place_ref.shape[0]
    slot_iota = lax.broadcasted_iota(jnp.int32, (tokens, slots), 1)
    for h in range(heads):
        select = jnp.where(slot_iota == place_ref[:, h : h + 1], 1.0, 0.0).astype(jnp.bfloat16)
        for n, ref in enumerate((dq_ref, dk_ref, dv_ref)):
            rows = home_ref[:, h * CAP : (h + 1) * CAP, n * DH : (n + 1) * DH].reshape(slots, DH)
            ref[:, h * DH : (h + 1) * DH] = jnp.dot(
                select, rows, preferred_element_type=jnp.float32
            ).astype(jnp.bfloat16)


def copies_to_all(block, axis):
    size = lax.axis_size(axis)
    return lax.all_to_all(
        jnp.broadcast_to(block[None], (size, *block.shape)), axis, 0, 0, tiled=True
    )


def after(value, earlier):
    return lax.optimization_barrier((value, earlier))[0]


def local(
    query_rows, key_rows, value_rows, saved_output, output_grad, out_weight, cluster_id, _slot
):
    tokens, width = query_rows.shape
    heads = cluster_id.shape[0]
    owners = lax.axis_size(SEQ)
    bf16 = jnp.bfloat16
    shape = jax.ShapeDtypeStruct

    full_grad = lax.all_gather(output_grad, HEAD, axis=1, tiled=True)
    weight_z = copies_to_all(out_weight, Z).reshape(-1, width)
    weight = lax.all_gather(weight_z, "x", axis=0, tiled=True)

    qkv = pl.pallas_call(
        pack_kernel,
        out_shape=shape((owners, heads * CAP, 3 * DH), bf16),
        compiler_params=PARAMS,
        name="pack_rows",
    )(cluster_id, query_rows, key_rows, value_rows)
    qkv = lax.all_to_all(after(qkv, weight_z), SEQ, 0, 0, tiled=True)

    cot, places = pl.pallas_call(
        cotangent_kernel,
        out_shape=(
            shape((owners * PAIR, DH), bf16),
            shape((tokens, 8), jnp.int32),
        ),
        compiler_params=PARAMS,
        name="cotangent_rows",
    )(cluster_id, full_grad, weight, saved_output)
    share = jnp.einsum("tc,td->cd", full_grad, saved_output, preferred_element_type=jnp.float32)
    share = after(share, weight)
    cot = after(cot, (share, qkv)).reshape(owners * PAIR // 2, 2, DH)
    cot = lax.all_to_all(cot, SEQ, 0, 0, tiled=True).reshape(owners * PAIR, DH)
    share = lax.psum_scatter(share, "x", scatter_dimension=0, tiled=True)
    weight_grad = pl.pallas_call(
        copy_kernel,
        out_shape=shape(out_weight.shape, jnp.float32),
        compiler_params=PARAMS,
        cost_estimate=EARLY,
        name="weight_grad",
    )(lax.psum_scatter(share, Z, scatter_dimension=0, tiled=True))

    grads = pl.pallas_call(
        attend_kernel,
        out_shape=shape((owners, heads * CAP, 3 * DH), bf16),
        scratch_shapes=[
            pltpu.VMEM((owners * CAP, owners * CAP), bf16),
            pltpu.VMEM((owners * CAP, owners * CAP), bf16),
        ],
        compiler_params=PARAMS,
        name="attend_cluster",
    )(qkv, cot)
    home = lax.all_to_all(grads, SEQ, 0, 0, tiled=True)
    dq, dk, dv = pl.pallas_call(
        unpack_kernel,
        out_shape=tuple(shape((tokens, width), bf16) for _ in range(3)),
        compiler_params=PARAMS,
        name="unpack_rows",
    )(home, places)
    return dq, dk, dv, weight_grad


def solution(mesh):
    n_head = mesh.devices.shape[1]
    grid = Mesh(mesh.devices.reshape(4, 4, 4, n_head // 2, 2), (*SEQ, *HEAD))
    rows, ids = P(SEQ, HEAD), P(HEAD, SEQ)
    return jax.shard_map(
        local,
        mesh=grid,
        in_specs=(rows,) * 6 + (ids,) * 2,
        out_specs=(rows,) * 4,
        check_vma=False,
    )
```

```python
import math

import jax
import jax.numpy as jnp
from jax import lax
from jax.experimental import pallas as pl
from jax.experimental.pallas import tpu as pltpu
from jax.sharding import Mesh
from jax.sharding import PartitionSpec as P

DH = 128
CAP = 16
PAIR = 2 * CAP + 2
BLOCK = 256
MASKED = -1e30
CONTRACT_LAST = (((1,), (1,)), ((), ()))
CONTRACT_FIRST = (((0,), (0,)), ((), ()))
SCALE = 1.0 / math.sqrt(DH)
LOG2_E = math.log2(math.e)
Z = ("z_hi", "z_lo")
SEQ = ("x", *Z)
HEAD = ("y", "core")
EARLY = pl.CostEstimate(flops=40_000_000_000, bytes_accessed=0, transcendentals=0)
PARAMS = pltpu.CompilerParams(vmem_limit_bytes=24 * 1024 * 1024)


def pair_places(ids, owners):
    heads, tokens = ids.shape
    earlier = (
        lax.broadcasted_iota(jnp.int32, (tokens, tokens), 0)
        < lax.broadcasted_iota(jnp.int32, (tokens, tokens), 1)
    ).astype(jnp.float32).astype(jnp.bfloat16)
    owner_iota = lax.broadcasted_iota(jnp.int32, (owners, tokens), 0)
    places = []
    for h in range(heads):
        onehot = jnp.where(owner_iota == ids[h : h + 1, :], 1.0, 0.0)
        before = jnp.dot(onehot.astype(jnp.bfloat16), earlier, preferred_element_type=jnp.float32)
        rank = jnp.sum(onehot * before, axis=0, keepdims=True)
        places.append((onehot, rank))
    return places


def pack_kernel(ids_ref, q_ref, k_ref, v_ref, out_ref):
    owners = out_ref.shape[0]
    ids = ids_ref[...]
    heads, tokens = ids.shape
    slots = owners * CAP
    slot_iota = lax.broadcasted_iota(jnp.int32, (slots, tokens), 0)
    for h, (_, rank) in enumerate(pair_places(ids, owners)):
        place = ids[h : h + 1, :] * CAP + rank.astype(jnp.int32)
        select = jnp.where(slot_iota == place, 1.0, 0.0).astype(jnp.bfloat16)
        for n, ref in enumerate((q_ref, k_ref, v_ref)):
            rows = jnp.dot(
                select, ref[:, h * DH : (h + 1) * DH], preferred_element_type=jnp.float32
            ).astype(jnp.bfloat16)
            out_ref[:, h * CAP : (h + 1) * CAP, n * DH : (n + 1) * DH] = rows.reshape(
                owners, CAP, DH
            )


def block_of(here_ref, back, other):
    y = lax.rem(here_ref[3] + 4 - back, 4)
    return y, here_ref[4] + other - 2 * other * here_ref[4]


def share_kernel(here_ref, saved_ref, *refs):
    *pairs, out_ref = refs
    half = saved_ref.shape[1]
    depth = out_ref.shape[3]
    for back, pair in enumerate(pairs):
        for other in range(2):
            x, core = block_of(here_ref, back, other)
            share = lax.dot_general(
                pair[other], saved_ref[...], CONTRACT_FIRST, preferred_element_type=jnp.float32
            )
            for n in range(half // depth):
                ahead = [
                    lax.rem(there + 4 - here_ref[axis], 4)
                    for axis, there in ((0, x), (2, n % 4), (1, core * 2 + n // 4))
                ]
                out_ref[ahead[0], ahead[1], ahead[2]] = share[n * depth : (n + 1) * depth, :]


def cotangent_kernel(here_ref, ids_ref, saved_ref, *refs):
    *blocks, out_ref, place_ref, weight_ref = refs
    parts, pairs = blocks[:4], blocks[4:]
    sent = out_ref.shape[0]
    owners = sent // PAIR
    ids = ids_ref[...]
    heads, tokens = ids.shape
    width = saved_ref.shape[1]
    for back, part in enumerate(parts):
        weight_ref[lax.rem(here_ref[0] + 4 - back, 4)] = part[...]
    cot = jnp.zeros((tokens, width), jnp.float32)
    for back, pair in enumerate(pairs):
        for other in range(2):
            x, core = block_of(here_ref, back, other)
            rows = pl.ds(pl.multiple_of(core * width, width), width)
            cot = cot + jnp.dot(
                pair[other], weight_ref[x, rows, :], preferred_element_type=jnp.float32
            )
    cot = cot.astype(jnp.bfloat16)
    row_iota = lax.broadcasted_iota(jnp.int32, (sent, tokens), 0)
    lane = lax.broadcasted_iota(jnp.int32, (tokens, DH), 1)
    row8 = lax.broadcasted_iota(jnp.int32, (8, tokens), 0)
    meta = jnp.zeros((owners, DH), jnp.float32)
    message = jnp.zeros((sent, DH), jnp.float32)
    places = pair_places(ids, owners)
    rank_rows = jnp.zeros((8, tokens), jnp.float32)
    place_rows = jnp.zeros((8, tokens), jnp.float32)
    for h, (_, rank) in enumerate(places):
        place = ids[h : h + 1, :].astype(jnp.float32) * CAP + rank
        rank_rows = jnp.where(row8 == h, rank, rank_rows)
        place_rows = jnp.where(row8 == h, place, place_rows)
    rank_columns = rank_rows.T
    place_ref[...] = place_rows.T.astype(jnp.int32)
    for h, (onehot, rank) in enumerate(places):
        g = cot[:, h * DH : (h + 1) * DH]
        o = saved_ref[:, h * DH : (h + 1) * DH]
        row_term = jnp.sum(g.astype(jnp.float32) * o.astype(jnp.float32), axis=1, keepdims=True)
        row_term = row_term.astype(jnp.bfloat16).astype(jnp.float32)
        where_to = rank_columns[:, h : h + 1].astype(jnp.int32) + 2 * CAP * h
        spread = jnp.where(lane == where_to, row_term, 0.0) + jnp.where(
            lane == where_to + CAP, 1.0, 0.0
        )
        meta = meta + jnp.dot(
            onehot.astype(jnp.bfloat16),
            spread.astype(jnp.bfloat16),
            preferred_element_type=jnp.float32,
        )
        place = ids[h : h + 1, :] * PAIR + h * CAP + rank.astype(jnp.int32)
        select = jnp.where(row_iota == place, 1.0, 0.0).astype(jnp.bfloat16)
        message = message + jnp.dot(select, g, preferred_element_type=jnp.float32)
    meta_lane = lax.broadcasted_iota(jnp.int32, (owners, DH), 1)
    meta = jnp.where((meta_lane & CAP) != 0, (1.0 - meta) * MASKED, meta)
    meta_row = lax.broadcasted_iota(jnp.int32, (sent, owners), 1) * PAIR + heads * CAP
    select = lax.broadcasted_iota(jnp.int32, (sent, owners), 0) == meta_row
    message = message + jnp.dot(
        jnp.where(select, 1.0, 0.0).astype(jnp.bfloat16),
        meta.astype(jnp.bfloat16),
        preferred_element_type=jnp.float32,
    )
    out_ref[...] = message.astype(jnp.bfloat16)


def attend_kernel(qkv_ref, g_ref, out_ref, prob_ref, score_ref):
    owners = qkv_ref.shape[0]
    heads = qkv_ref.shape[1] // CAP
    slots = owners * CAP
    meta = jnp.concatenate(
        [
            jnp.broadcast_to(
                g_ref[first : first + 2, :].astype(jnp.float32)[:1], (CAP, DH)
            )
            for first in range(heads * CAP, owners * PAIR, PAIR)
        ],
        axis=0,
    )
    lane = lax.broadcasted_iota(jnp.int32, (slots, DH), 1)
    rank = lax.broadcasted_iota(jnp.int32, (slots, DH), 0) & (CAP - 1)
    later = lax.broadcasted_iota(jnp.int32, (BLOCK, BLOCK), 0) > lax.broadcasted_iota(
        jnp.int32, (BLOCK, BLOCK), 1
    )

    def rows_of(h, n):
        return qkv_ref[:, h * CAP : (h + 1) * CAP, n * DH : (n + 1) * DH].reshape(slots, DH)

    for h in range(heads):
        q, k, v = (rows_of(h, n) for n in range(3))
        g = jnp.concatenate(
            [g_ref[n : n + CAP, :] for n in range(h * CAP, owners * PAIR, PAIR)], axis=0
        )
        term_lanes = (lane >= 2 * CAP * h) & (lane < 2 * CAP * h + CAP)
        bias_lanes = (lane >= 2 * CAP * h + CAP) & (lane < 2 * CAP * (h + 1))
        own = jnp.where((lane & (CAP - 1)) == rank, meta, 0.0)
        extra = jnp.where(term_lanes | bias_lanes, own, 0.0).astype(jnp.bfloat16)
        minus_one = jnp.where(term_lanes, -1.0, 0.0).astype(jnp.bfloat16)
        one = jnp.where(bias_lanes, 1.0, 0.0).astype(jnp.bfloat16)
        k_turned = k.T
        q_wide = jnp.concatenate([q, one], axis=1)
        k_wide = jnp.concatenate([k, extra], axis=1)
        g_wide = jnp.concatenate([g, extra], axis=1)
        v_wide = jnp.concatenate([v, minus_one], axis=1)
        for start in range(0, slots, BLOCK):
            stop = start + BLOCK
            scores = lax.dot_general(
                k_wide[:stop], q_wide[start:stop], CONTRACT_LAST,
                preferred_element_type=jnp.float32,
            )
            last = jnp.where(later, MASKED, scores[start:stop])
            if start:
                scores = jnp.concatenate([scores[:start], last], axis=0)
            else:
                scores = last
            row_max = jnp.max(scores, axis=0, keepdims=True)
            exponent = jnp.exp2((scores - row_max) * (SCALE * LOG2_E))
            inverse = 1.0 / jnp.sum(exponent, axis=0, keepdims=True)
            grad_prob = lax.dot_general(
                v_wide[:stop], g_wide[start:stop], CONTRACT_LAST,
                preferred_element_type=jnp.float32,
            )
            grad_score = (exponent * (inverse * SCALE) * grad_prob).astype(jnp.bfloat16)
            prob_ref[:stop, start:stop] = (exponent * inverse).astype(jnp.bfloat16)
            score_ref[:stop, start:stop] = grad_score
        for start in range(0, slots, BLOCK):
            stop = start + BLOCK
            grad_query = jnp.dot(
                k_turned[:, :stop], score_ref[:stop, start:stop], preferred_element_type=jnp.float32
            ).T
            out_ref[start // CAP : stop // CAP, h * CAP : (h + 1) * CAP, 0:DH] = (
                grad_query.astype(jnp.bfloat16).reshape(BLOCK // CAP, CAP, DH)
            )
            for n, ref, other in ((1, score_ref, q), (2, prob_ref, g)):
                grad = jnp.dot(
                    ref[start:stop, start:], other[start:], preferred_element_type=jnp.float32
                )
                out_ref[
                    start // CAP : stop // CAP, h * CAP : (h + 1) * CAP, n * DH : (n + 1) * DH
                ] = grad.astype(jnp.bfloat16).reshape(BLOCK // CAP, CAP, DH)


def add_kernel(own_ref, *refs):
    *others, sum_ref, sent_ref = refs
    total = own_ref[...]
    for ref in others:
        total = total + ref[...].astype(jnp.float32)
    sum_ref[...] = total[0]
    sent_ref[...] = total.astype(jnp.bfloat16)


def add_last_kernel(own_ref, *refs):
    *others, sum_ref = refs
    sum_ref[...] = own_ref[...] + sum(ref[...].astype(jnp.float32) for ref in others)


def unpack_kernel(home_ref, place_ref, dq_ref, dk_ref, dv_ref):
    owners = home_ref.shape[0]
    heads = home_ref.shape[1] // CAP
    slots = owners * CAP
    tokens = place_ref.shape[0]
    slot_iota = lax.broadcasted_iota(jnp.int32, (tokens, slots), 1)
    for h in range(heads):
        select = jnp.where(slot_iota == place_ref[:, h : h + 1], 1.0, 0.0).astype(jnp.bfloat16)
        for n, ref in enumerate((dq_ref, dk_ref, dv_ref)):
            rows = home_ref[:, h * CAP : (h + 1) * CAP, n * DH : (n + 1) * DH].reshape(slots, DH)
            ref[:, h * DH : (h + 1) * DH] = jnp.dot(
                select, rows, preferred_element_type=jnp.float32
            ).astype(jnp.bfloat16)


def copies_to_all(block, axis):
    size = lax.axis_size(axis)
    return lax.all_to_all(
        jnp.broadcast_to(block[None], (size, *block.shape)), axis, 0, 0, tiled=True
    )


def forward(block, axis, shift):
    size = lax.axis_size(axis)
    return lax.ppermute(block, axis, [(i, (i + shift) % size) for i in range(size)])


def scatter_sum(blocks, axis):
    total = blocks[0]
    for n in range(1, lax.axis_size(axis)):
        total = total + forward(blocks[n].astype(jnp.bfloat16), axis, n).astype(jnp.float32)
    return total


def after(value, earlier):
    return lax.optimization_barrier((value, earlier))[0]


def local(
    query_rows, key_rows, value_rows, saved_output, output_grad, out_weight, cluster_id, _slot
):
    tokens, width = query_rows.shape
    heads = cluster_id.shape[0]
    owners = lax.axis_size(SEQ)
    bf16 = jnp.bfloat16
    shape = jax.ShapeDtypeStruct

    smem, vmem = (pl.BlockSpec(memory_space=space) for space in (pltpu.SMEM, pltpu.VMEM))
    here = jnp.stack([lax.axis_index(axis) for axis in (*SEQ, *HEAD)]).astype(jnp.int32)

    weight_z = copies_to_all(out_weight, Z).reshape(-1, width)
    qkv = pl.pallas_call(
        pack_kernel,
        out_shape=shape((owners, heads * CAP, 3 * DH), bf16),
        compiler_params=PARAMS,
        name="pack_rows",
    )(cluster_id, query_rows, key_rows, value_rows)
    pair = jnp.stack([output_grad, forward(output_grad, "core", 1)])
    qkv = lax.all_to_all(after(qkv, (weight_z, pair)), SEQ, 0, 0, tiled=True)

    pairs = [pair] + [forward(pair, "y", n) for n in range(1, lax.axis_size("y"))]
    parts = [weight_z] + [forward(weight_z, "x", n) for n in range(1, lax.axis_size("x"))]
    cot, places = pl.pallas_call(
        cotangent_kernel,
        out_shape=(
            shape((owners * PAIR, DH), bf16),
            shape((tokens, 8), jnp.int32),
        ),
        in_specs=[smem] + [vmem] * (2 + len(parts) + len(pairs)),
        scratch_shapes=[pltpu.VMEM((len(parts), *weight_z.shape), bf16)],
        compiler_params=PARAMS,
        name="cotangent_rows",
    )(here, cluster_id, saved_output, *parts, *pairs)
    share = pl.pallas_call(
        share_kernel,
        out_shape=shape((4, 4, 4, out_weight.shape[0], width), jnp.float32),
        in_specs=[smem] + [vmem] * (1 + len(pairs)),
        compiler_params=PARAMS,
        name="weight_share",
    )(here, after(saved_output, places), *pairs)
    share = scatter_sum(share, "x")
    moved = [forward(share[n].astype(bf16), "z_lo", n) for n in range(1, 4)]
    cot, own, qkv = lax.optimization_barrier((cot, share[0], qkv))
    cot = cot.reshape(owners * PAIR // 2, 2, DH)
    cot = lax.all_to_all(cot, SEQ, 0, 0, tiled=True).reshape(owners * PAIR, DH)
    own, share = pl.pallas_call(
        add_kernel,
        out_shape=(shape(own.shape[1:], jnp.float32), shape(own.shape, bf16)),
        compiler_params=PARAMS,
        cost_estimate=EARLY,
        name="add_along_z_lo",
    )(own, *moved)
    moved = [forward(share[n], "z_hi", n) for n in range(1, 4)]
    weight_grad = pl.pallas_call(
        add_last_kernel,
        out_shape=shape(own.shape, jnp.float32),
        compiler_params=PARAMS,
        cost_estimate=pl.CostEstimate(flops=50_000_000_000, bytes_accessed=0, transcendentals=0),
        name="add_along_z_hi",
    )(own, *moved)

    grads = pl.pallas_call(
        attend_kernel,
        out_shape=shape((owners, heads * CAP, 3 * DH), bf16),
        scratch_shapes=[
            pltpu.VMEM((owners * CAP, owners * CAP), bf16),
            pltpu.VMEM((owners * CAP, owners * CAP), bf16),
        ],
        compiler_params=PARAMS,
        name="attend_cluster",
    )(qkv, cot)
    home = lax.all_to_all(grads, SEQ, 0, 0, tiled=True)
    dq, dk, dv = pl.pallas_call(
        unpack_kernel,
        out_shape=tuple(shape((tokens, width), bf16) for _ in range(3)),
        compiler_params=PARAMS,
        name="unpack_rows",
    )(home, places)
    return dq, dk, dv, weight_grad


def solution(mesh):
    n_head = mesh.devices.shape[1]
    grid = Mesh(mesh.devices.reshape(4, 4, 4, n_head // 2, 2), (*SEQ, *HEAD))
    rows, ids = P(SEQ, HEAD), P(HEAD, SEQ)
    return jax.shard_map(
        local,
        mesh=grid,
        in_specs=(rows,) * 6 + (ids,) * 2,
        out_specs=(rows,) * 4,
        check_vma=False,
    )
```

```python
import math

import jax
import jax.numpy as jnp
from jax import lax
from jax.experimental import pallas as pl
from jax.experimental.pallas import tpu as pltpu
from jax.sharding import Mesh
from jax.sharding import PartitionSpec as P

DH = 128
CAP = 16
PAIR = 2 * CAP + 2
BLOCK = 256
MASKED = -1e30
CONTRACT_LAST = (((1,), (1,)), ((), ()))
CONTRACT_FIRST = (((0,), (0,)), ((), ()))
SCALE = 1.0 / math.sqrt(DH)
LOG2_E = math.log2(math.e)
Z = ("z_hi", "z_lo")
SEQ = ("x", *Z)
HEAD = ("y", "core")
EARLY = pl.CostEstimate(flops=90_000_000_000, bytes_accessed=0, transcendentals=0)
PARAMS = pltpu.CompilerParams(vmem_limit_bytes=24 * 1024 * 1024)


def pair_places(ids, owners):
    heads, tokens = ids.shape
    earlier = (
        lax.broadcasted_iota(jnp.int32, (tokens, tokens), 0)
        < lax.broadcasted_iota(jnp.int32, (tokens, tokens), 1)
    ).astype(jnp.float32).astype(jnp.bfloat16)
    owner_iota = lax.broadcasted_iota(jnp.int32, (owners, tokens), 0)
    places = []
    for h in range(heads):
        onehot = jnp.where(owner_iota == ids[h : h + 1, :], 1.0, 0.0)
        before = jnp.dot(onehot.astype(jnp.bfloat16), earlier, preferred_element_type=jnp.float32)
        rank = jnp.sum(onehot * before, axis=0, keepdims=True)
        places.append((onehot, rank))
    return places


def pack_kernel(ids_ref, q_ref, k_ref, v_ref, out_ref):
    owners = out_ref.shape[0]
    ids = ids_ref[...]
    heads, tokens = ids.shape
    slots = owners * CAP
    slot_iota = lax.broadcasted_iota(jnp.int32, (slots, tokens), 0)
    for h, (_, rank) in enumerate(pair_places(ids, owners)):
        place = ids[h : h + 1, :] * CAP + rank.astype(jnp.int32)
        select = jnp.where(slot_iota == place, 1.0, 0.0).astype(jnp.bfloat16)
        for n, ref in enumerate((q_ref, k_ref, v_ref)):
            rows = jnp.dot(
                select, ref[:, h * DH : (h + 1) * DH], preferred_element_type=jnp.float32
            ).astype(jnp.bfloat16)
            out_ref[:, h * CAP : (h + 1) * CAP, n * DH : (n + 1) * DH] = rows.reshape(
                owners, CAP, DH
            )


def block_of(here_ref, back, other):
    y = lax.rem(here_ref[3] + 4 - back, 4)
    return y, here_ref[4] + other - 2 * other * here_ref[4]


def share_kernel(here_ref, saved_ref, *refs):
    *pairs, out_ref = refs
    half = saved_ref.shape[1]
    depth = out_ref.shape[3]
    for back, pair in enumerate(pairs):
        for other in range(2):
            x, core = block_of(here_ref, back, other)
            share = lax.dot_general(
                pair[other], saved_ref[...], CONTRACT_FIRST, preferred_element_type=jnp.float32
            )
            for n in range(half // depth):
                ahead = [
                    lax.rem(there + 4 - here_ref[axis], 4)
                    for axis, there in ((0, x), (2, n % 4), (1, core * 2 + n // 4))
                ]
                out_ref[ahead[0], ahead[1], ahead[2]] = share[n * depth : (n + 1) * depth, :]


def cotangent_kernel(here_ref, ids_ref, saved_ref, *refs):
    *blocks, out_ref, place_ref, weight_ref = refs
    parts, pairs = blocks[:4], blocks[4:]
    sent = out_ref.shape[0]
    owners = sent // PAIR
    ids = ids_ref[...]
    heads, tokens = ids.shape
    width = saved_ref.shape[1]
    for back, part in enumerate(parts):
        weight_ref[lax.rem(here_ref[0] + 4 - back, 4)] = part[...]
    cot = jnp.zeros((tokens, width), jnp.float32)
    for back, pair in enumerate(pairs):
        for other in range(2):
            x, core = block_of(here_ref, back, other)
            rows = pl.ds(pl.multiple_of(core * width, width), width)
            cot = cot + jnp.dot(
                pair[other], weight_ref[x, rows, :], preferred_element_type=jnp.float32
            )
    cot = cot.astype(jnp.bfloat16)
    row_iota = lax.broadcasted_iota(jnp.int32, (sent, tokens), 0)
    lane = lax.broadcasted_iota(jnp.int32, (tokens, DH), 1)
    row8 = lax.broadcasted_iota(jnp.int32, (8, tokens), 0)
    meta = jnp.zeros((owners, DH), jnp.float32)
    message = jnp.zeros((sent, DH), jnp.float32)
    places = pair_places(ids, owners)
    rank_rows = jnp.zeros((8, tokens), jnp.float32)
    place_rows = jnp.zeros((8, tokens), jnp.float32)
    for h, (_, rank) in enumerate(places):
        place = ids[h : h + 1, :].astype(jnp.float32) * CAP + rank
        rank_rows = jnp.where(row8 == h, rank, rank_rows)
        place_rows = jnp.where(row8 == h, place, place_rows)
    rank_columns = rank_rows.T
    place_ref[...] = place_rows.T.astype(jnp.int32)
    for h, (onehot, rank) in enumerate(places):
        g = cot[:, h * DH : (h + 1) * DH]
        o = saved_ref[:, h * DH : (h + 1) * DH]
        row_term = jnp.sum(g.astype(jnp.float32) * o.astype(jnp.float32), axis=1, keepdims=True)
        row_term = row_term.astype(jnp.bfloat16).astype(jnp.float32)
        where_to = rank_columns[:, h : h + 1].astype(jnp.int32) + 2 * CAP * h
        spread = jnp.where(lane == where_to, row_term, 0.0) + jnp.where(
            lane == where_to + CAP, 1.0, 0.0
        )
        meta = meta + jnp.dot(
            onehot.astype(jnp.bfloat16),
            spread.astype(jnp.bfloat16),
            preferred_element_type=jnp.float32,
        )
        place = ids[h : h + 1, :] * PAIR + h * CAP + rank.astype(jnp.int32)
        select = jnp.where(row_iota == place, 1.0, 0.0).astype(jnp.bfloat16)
        message = message + jnp.dot(select, g, preferred_element_type=jnp.float32)
    meta_lane = lax.broadcasted_iota(jnp.int32, (owners, DH), 1)
    meta = jnp.where((meta_lane & CAP) != 0, (1.0 - meta) * MASKED, meta)
    meta_row = lax.broadcasted_iota(jnp.int32, (sent, owners), 1) * PAIR + heads * CAP
    select = lax.broadcasted_iota(jnp.int32, (sent, owners), 0) == meta_row
    message = message + jnp.dot(
        jnp.where(select, 1.0, 0.0).astype(jnp.bfloat16),
        meta.astype(jnp.bfloat16),
        preferred_element_type=jnp.float32,
    )
    out_ref[...] = message.astype(jnp.bfloat16)


def attend_kernel(qkv_ref, g_ref, out_ref, prob_ref, score_ref):
    owners = qkv_ref.shape[0]
    heads = qkv_ref.shape[1] // CAP
    slots = owners * CAP
    meta = jnp.concatenate(
        [
            jnp.broadcast_to(
                g_ref[first : first + 2, :].astype(jnp.float32)[:1], (CAP, DH)
            )
            for first in range(heads * CAP, owners * PAIR, PAIR)
        ],
        axis=0,
    )
    lane = lax.broadcasted_iota(jnp.int32, (slots, DH), 1)
    rank = lax.broadcasted_iota(jnp.int32, (slots, DH), 0) & (CAP - 1)
    later = lax.broadcasted_iota(jnp.int32, (BLOCK, BLOCK), 0) > lax.broadcasted_iota(
        jnp.int32, (BLOCK, BLOCK), 1
    )

    def rows_of(h, n):
        return qkv_ref[:, h * CAP : (h + 1) * CAP, n * DH : (n + 1) * DH].reshape(slots, DH)

    for h in range(heads):
        q, k, v = (rows_of(h, n) for n in range(3))
        g = jnp.concatenate(
            [g_ref[n : n + CAP, :] for n in range(h * CAP, owners * PAIR, PAIR)], axis=0
        )
        term_lanes = (lane >= 2 * CAP * h) & (lane < 2 * CAP * h + CAP)
        bias_lanes = (lane >= 2 * CAP * h + CAP) & (lane < 2 * CAP * (h + 1))
        own = jnp.where((lane & (CAP - 1)) == rank, meta, 0.0)
        extra = jnp.where(term_lanes | bias_lanes, own, 0.0).astype(jnp.bfloat16)
        minus_one = jnp.where(term_lanes, -1.0, 0.0).astype(jnp.bfloat16)
        one = jnp.where(bias_lanes, 1.0, 0.0).astype(jnp.bfloat16)
        k_turned = k.T
        q_wide = jnp.concatenate([q, one], axis=1)
        k_wide = jnp.concatenate([k, extra], axis=1)
        g_wide = jnp.concatenate([g, extra], axis=1)
        v_wide = jnp.concatenate([v, minus_one], axis=1)
        for start in range(0, slots, BLOCK):
            stop = start + BLOCK
            scores = lax.dot_general(
                k_wide[:stop], q_wide[start:stop], CONTRACT_LAST,
                preferred_element_type=jnp.float32,
            )
            last = jnp.where(later, MASKED, scores[start:stop])
            if start:
                scores = jnp.concatenate([scores[:start], last], axis=0)
            else:
                scores = last
            row_max = jnp.max(scores, axis=0, keepdims=True)
            exponent = jnp.exp2((scores - row_max) * (SCALE * LOG2_E))
            inverse = 1.0 / jnp.sum(exponent, axis=0, keepdims=True)
            grad_prob = lax.dot_general(
                v_wide[:stop], g_wide[start:stop], CONTRACT_LAST,
                preferred_element_type=jnp.float32,
            )
            grad_score = (exponent * (inverse * SCALE) * grad_prob).astype(jnp.bfloat16)
            prob_ref[:stop, start:stop] = (exponent * inverse).astype(jnp.bfloat16)
            score_ref[:stop, start:stop] = grad_score
        for start in range(0, slots, BLOCK):
            stop = start + BLOCK
            grad_query = jnp.dot(
                k_turned[:, :stop], score_ref[:stop, start:stop], preferred_element_type=jnp.float32
            ).T
            out_ref[start // CAP : stop // CAP, h * CAP : (h + 1) * CAP, 0:DH] = (
                grad_query.astype(jnp.bfloat16).reshape(BLOCK // CAP, CAP, DH)
            )
            for n, ref, other in ((1, score_ref, q), (2, prob_ref, g)):
                grad = jnp.dot(
                    ref[start:stop, start:], other[start:], preferred_element_type=jnp.float32
                )
                out_ref[
                    start // CAP : stop // CAP, h * CAP : (h + 1) * CAP, n * DH : (n + 1) * DH
                ] = grad.astype(jnp.bfloat16).reshape(BLOCK // CAP, CAP, DH)


def add_kernel(own_ref, *refs):
    *others, sum_ref, sent_ref = refs
    total = own_ref[...]
    for ref in others:
        total = total + ref[...].astype(jnp.float32)
    sum_ref[...] = total[0]
    sent_ref[...] = total.astype(jnp.bfloat16)


def add_last_kernel(own_ref, *refs):
    *others, sum_ref = refs
    sum_ref[...] = own_ref[...] + sum(ref[...].astype(jnp.float32) for ref in others)


def unpack_kernel(home_ref, place_ref, dq_ref, dk_ref, dv_ref):
    owners = home_ref.shape[0]
    heads = home_ref.shape[1] // CAP
    slots = owners * CAP
    tokens = place_ref.shape[0]
    slot_iota = lax.broadcasted_iota(jnp.int32, (tokens, slots), 1)
    for h in range(heads):
        select = jnp.where(slot_iota == place_ref[:, h : h + 1], 1.0, 0.0).astype(jnp.bfloat16)
        rows = home_ref[:, h * CAP : (h + 1) * CAP, :].reshape(slots, 3 * DH)
        rows = jnp.dot(select, rows, preferred_element_type=jnp.float32).astype(jnp.bfloat16)
        for n, ref in enumerate((dq_ref, dk_ref, dv_ref)):
            ref[:, h * DH : (h + 1) * DH] = rows[:, n * DH : (n + 1) * DH]


def copies_to_all(block, axis):
    size = lax.axis_size(axis)
    return lax.all_to_all(
        jnp.broadcast_to(block[None], (size, *block.shape)), axis, 0, 0, tiled=True
    )


def forward(block, axis, shift):
    size = lax.axis_size(axis)
    return lax.ppermute(block, axis, [(i, (i + shift) % size) for i in range(size)])


def scatter_sum(blocks, axis):
    total = blocks[0]
    for n in range(1, lax.axis_size(axis)):
        total = total + forward(blocks[n].astype(jnp.bfloat16), axis, n).astype(jnp.float32)
    return total


def after(value, earlier):
    return lax.optimization_barrier((value, earlier))[0]


def local(
    query_rows, key_rows, value_rows, saved_output, output_grad, out_weight, cluster_id, _slot
):
    tokens, width = query_rows.shape
    heads = cluster_id.shape[0]
    owners = lax.axis_size(SEQ)
    bf16 = jnp.bfloat16
    shape = jax.ShapeDtypeStruct

    smem, vmem = (pl.BlockSpec(memory_space=space) for space in (pltpu.SMEM, pltpu.VMEM))
    here = jnp.stack([lax.axis_index(axis) for axis in (*SEQ, *HEAD)]).astype(jnp.int32)

    weight_z = copies_to_all(out_weight, Z).reshape(-1, width)
    qkv = pl.pallas_call(
        pack_kernel,
        out_shape=shape((owners, heads * CAP, 3 * DH), bf16),
        compiler_params=PARAMS,
        name="pack_rows",
    )(cluster_id, query_rows, key_rows, value_rows)
    pair = jnp.stack([output_grad, forward(output_grad, "core", 1)])
    qkv = lax.all_to_all(after(qkv, (weight_z, pair)), SEQ, 0, 0, tiled=True)

    pairs = [pair] + [forward(pair, "y", n) for n in range(1, lax.axis_size("y"))]
    parts = [weight_z] + [forward(weight_z, "x", n) for n in range(1, lax.axis_size("x"))]
    cot, places = pl.pallas_call(
        cotangent_kernel,
        out_shape=(
            shape((owners * PAIR, DH), bf16),
            shape((tokens, 8), jnp.int32),
        ),
        in_specs=[smem] + [vmem] * (2 + len(parts) + len(pairs)),
        scratch_shapes=[pltpu.VMEM((len(parts), *weight_z.shape), bf16)],
        compiler_params=PARAMS,
        name="cotangent_rows",
    )(here, cluster_id, saved_output, *parts, *pairs)
    share = pl.pallas_call(
        share_kernel,
        out_shape=shape((4, 4, 4, out_weight.shape[0], width), jnp.float32),
        in_specs=[smem] + [vmem] * (1 + len(pairs)),
        compiler_params=PARAMS,
        name="weight_share",
    )(here, after(saved_output, places), *pairs)
    share = scatter_sum(share, "x")
    moved = [forward(share[n].astype(bf16), "z_lo", n) for n in range(1, 4)]
    cot, own, qkv = lax.optimization_barrier((cot, share[0], qkv))
    cot = cot.reshape(owners * PAIR // 2, 2, DH)
    cot = lax.all_to_all(cot, SEQ, 0, 0, tiled=True).reshape(owners * PAIR, DH)
    own, share = pl.pallas_call(
        add_kernel,
        out_shape=(shape(own.shape[1:], jnp.float32), shape(own.shape, bf16)),
        compiler_params=PARAMS,
        cost_estimate=EARLY,
        name="add_along_z_lo",
    )(own, *moved)
    moved = [forward(share[n], "z_hi", n) for n in range(1, 4)]
    grads = pl.pallas_call(
        attend_kernel,
        out_shape=shape((owners, heads * CAP, 3 * DH), bf16),
        scratch_shapes=[
            pltpu.VMEM((owners * CAP, owners * CAP), bf16),
            pltpu.VMEM((owners * CAP, owners * CAP), bf16),
        ],
        compiler_params=PARAMS,
        name="attend_cluster",
    )(qkv, cot)
    home = lax.all_to_all(grads, SEQ, 0, 0, tiled=True)
    dq, dk, dv = pl.pallas_call(
        unpack_kernel,
        out_shape=tuple(shape((tokens, width), bf16) for _ in range(3)),
        compiler_params=PARAMS,
        name="unpack_rows",
    )(home, places)
    own, moved, dq = lax.optimization_barrier((own, moved, dq))
    weight_grad = pl.pallas_call(
        add_last_kernel,
        out_shape=shape(own.shape, jnp.float32),
        compiler_params=PARAMS,
        name="add_along_z_hi",
    )(own, *moved)
    return dq, dk, dv, weight_grad


def solution(mesh):
    n_head = mesh.devices.shape[1]
    grid = Mesh(mesh.devices.reshape(4, 4, 4, n_head // 2, 2), (*SEQ, *HEAD))
    rows, ids = P(SEQ, HEAD), P(HEAD, SEQ)
    return jax.shard_map(
        local,
        mesh=grid,
        in_specs=(rows,) * 6 + (ids,) * 2,
        out_specs=(rows,) * 4,
        check_vma=False,
    )
```

```python
import math

import jax
import jax.numpy as jnp
from jax import lax
from jax.experimental import pallas as pl
from jax.experimental.pallas import tpu as pltpu
from jax.sharding import Mesh
from jax.sharding import PartitionSpec as P

DH = 128
CAP = 16
PAIR = 2 * CAP + 2
BLOCK = 256
MASKED = -1e30
CONTRACT_LAST = (((1,), (1,)), ((), ()))
CONTRACT_FIRST = (((0,), (0,)), ((), ()))
SCALE = 1.0 / math.sqrt(DH)
LOG2_E = math.log2(math.e)
Z = ("z_hi", "z_lo")
SEQ = ("x", *Z)
HEAD = ("y", "core")
EARLY = pl.CostEstimate(flops=90_000_000_000, bytes_accessed=0, transcendentals=0)
PARAMS = pltpu.CompilerParams(vmem_limit_bytes=24 * 1024 * 1024)


def pair_places(ids, owners):
    heads, tokens = ids.shape
    earlier = (
        lax.broadcasted_iota(jnp.int32, (tokens, tokens), 0)
        < lax.broadcasted_iota(jnp.int32, (tokens, tokens), 1)
    ).astype(jnp.float32).astype(jnp.bfloat16)
    owner_iota = lax.broadcasted_iota(jnp.int32, (owners, tokens), 0)
    places = []
    for h in range(heads):
        onehot = jnp.where(owner_iota == ids[h : h + 1, :], 1.0, 0.0)
        before = jnp.dot(onehot.astype(jnp.bfloat16), earlier, preferred_element_type=jnp.float32)
        rank = jnp.sum(onehot * before, axis=0, keepdims=True)
        places.append((onehot, rank))
    return places


def pack_kernel(ids_ref, q_ref, k_ref, v_ref, out_ref):
    owners = out_ref.shape[0]
    ids = ids_ref[...]
    heads, tokens = ids.shape
    slots = owners * CAP
    slot_iota = lax.broadcasted_iota(jnp.int32, (slots, tokens), 0)
    for h, (_, rank) in enumerate(pair_places(ids, owners)):
        place = ids[h : h + 1, :] * CAP + rank.astype(jnp.int32)
        select = jnp.where(slot_iota == place, 1.0, 0.0).astype(jnp.bfloat16)
        for n, ref in enumerate((q_ref, k_ref, v_ref)):
            rows = jnp.dot(
                select, ref[:, h * DH : (h + 1) * DH], preferred_element_type=jnp.float32
            ).astype(jnp.bfloat16)
            out_ref[:, h * CAP : (h + 1) * CAP, n * DH : (n + 1) * DH] = rows.reshape(
                owners, CAP, DH
            )


def block_of(here_ref, back, other):
    y = lax.rem(here_ref[3] + 4 - back, 4)
    return y, here_ref[4] + other - 2 * other * here_ref[4]


def share_kernel(here_ref, saved_ref, *refs):
    *pairs, out_ref = refs
    half = saved_ref.shape[1]
    depth = out_ref.shape[3]
    for back, pair in enumerate(pairs):
        for other in range(2):
            x, core = block_of(here_ref, back, other)
            share = lax.dot_general(
                pair[other], saved_ref[...], CONTRACT_FIRST, preferred_element_type=jnp.float32
            )
            for n in range(half // depth):
                ahead = [
                    lax.rem(there + 4 - here_ref[axis], 4)
                    for axis, there in ((0, x), (2, n % 4), (1, core * 2 + n // 4))
                ]
                out_ref[ahead[0], ahead[1], ahead[2]] = share[n * depth : (n + 1) * depth, :]


def cotangent_kernel(here_ref, ids_ref, saved_ref, *refs):
    *blocks, out_ref, place_ref, weight_ref = refs
    parts, pairs = blocks[:4], blocks[4:]
    sent = out_ref.shape[0]
    owners = sent // PAIR
    ids = ids_ref[...]
    heads, tokens = ids.shape
    width = saved_ref.shape[1]
    for back, part in enumerate(parts):
        weight_ref[lax.rem(here_ref[0] + 4 - back, 4)] = part[...]
    cot = jnp.zeros((tokens, width), jnp.float32)
    for back, pair in enumerate(pairs):
        for other in range(2):
            x, core = block_of(here_ref, back, other)
            rows = pl.ds(pl.multiple_of(core * width, width), width)
            cot = cot + jnp.dot(
                pair[other], weight_ref[x, rows, :], preferred_element_type=jnp.float32
            )
    cot = cot.astype(jnp.bfloat16)
    row_iota = lax.broadcasted_iota(jnp.int32, (sent, tokens), 0)
    lane = lax.broadcasted_iota(jnp.int32, (tokens, DH), 1)
    row8 = lax.broadcasted_iota(jnp.int32, (8, tokens), 0)
    meta = jnp.zeros((owners, DH), jnp.float32)
    message = jnp.zeros((sent, DH), jnp.float32)
    places = pair_places(ids, owners)
    rank_rows = jnp.zeros((8, tokens), jnp.float32)
    place_rows = jnp.zeros((8, tokens), jnp.float32)
    for h, (_, rank) in enumerate(places):
        place = ids[h : h + 1, :].astype(jnp.float32) * CAP + rank
        rank_rows = jnp.where(row8 == h, rank, rank_rows)
        place_rows = jnp.where(row8 == h, place, place_rows)
    rank_columns = rank_rows.T
    place_ref[...] = place_rows.T.astype(jnp.int32)
    for h, (onehot, rank) in enumerate(places):
        g = cot[:, h * DH : (h + 1) * DH]
        o = saved_ref[:, h * DH : (h + 1) * DH]
        row_term = jnp.sum(g.astype(jnp.float32) * o.astype(jnp.float32), axis=1, keepdims=True)
        row_term = row_term.astype(jnp.bfloat16).astype(jnp.float32)
        where_to = rank_columns[:, h : h + 1].astype(jnp.int32) + 2 * CAP * h
        spread = jnp.where(lane == where_to, row_term, 0.0) + jnp.where(
            lane == where_to + CAP, 1.0, 0.0
        )
        meta = meta + jnp.dot(
            onehot.astype(jnp.bfloat16),
            spread.astype(jnp.bfloat16),
            preferred_element_type=jnp.float32,
        )
        place = ids[h : h + 1, :] * PAIR + h * CAP + rank.astype(jnp.int32)
        select = jnp.where(row_iota == place, 1.0, 0.0).astype(jnp.bfloat16)
        message = message + jnp.dot(select, g, preferred_element_type=jnp.float32)
    meta_lane = lax.broadcasted_iota(jnp.int32, (owners, DH), 1)
    meta = jnp.where((meta_lane & CAP) != 0, (1.0 - meta) * MASKED, meta)
    meta_row = lax.broadcasted_iota(jnp.int32, (sent, owners), 1) * PAIR + heads * CAP
    select = lax.broadcasted_iota(jnp.int32, (sent, owners), 0) == meta_row
    message = message + jnp.dot(
        jnp.where(select, 1.0, 0.0).astype(jnp.bfloat16),
        meta.astype(jnp.bfloat16),
        preferred_element_type=jnp.float32,
    )
    out_ref[...] = message.astype(jnp.bfloat16)


def attend_kernel(qkv_ref, g_ref, out_ref, prob_ref, score_ref):
    owners = qkv_ref.shape[0]
    heads = qkv_ref.shape[1] // CAP
    slots = owners * CAP
    meta = jnp.concatenate(
        [
            jnp.broadcast_to(
                g_ref[first : first + 2, :].astype(jnp.float32)[:1], (CAP, DH)
            )
            for first in range(heads * CAP, owners * PAIR, PAIR)
        ],
        axis=0,
    )
    lane = lax.broadcasted_iota(jnp.int32, (slots, DH), 1)
    rank = lax.broadcasted_iota(jnp.int32, (slots, DH), 0) & (CAP - 1)
    later = lax.broadcasted_iota(jnp.int32, (BLOCK, BLOCK), 0) > lax.broadcasted_iota(
        jnp.int32, (BLOCK, BLOCK), 1
    )

    def rows_of(h, n):
        return qkv_ref[:, h * CAP : (h + 1) * CAP, n * DH : (n + 1) * DH].reshape(slots, DH)

    for h in range(heads):
        q, k, v = (rows_of(h, n) for n in range(3))
        g = jnp.concatenate(
            [g_ref[n : n + CAP, :] for n in range(h * CAP, owners * PAIR, PAIR)], axis=0
        )
        term_lanes = (lane >= 2 * CAP * h) & (lane < 2 * CAP * h + CAP)
        bias_lanes = (lane >= 2 * CAP * h + CAP) & (lane < 2 * CAP * (h + 1))
        own = jnp.where((lane & (CAP - 1)) == rank, meta, 0.0)
        extra = jnp.where(term_lanes | bias_lanes, own, 0.0).astype(jnp.bfloat16)
        minus_one = jnp.where(term_lanes, -1.0, 0.0).astype(jnp.bfloat16)
        one = jnp.where(bias_lanes, 1.0, 0.0).astype(jnp.bfloat16)
        k_turned = k.T
        q_wide = jnp.concatenate([q, one], axis=1)
        k_wide = jnp.concatenate([k, extra], axis=1)
        g_wide = jnp.concatenate([g, extra], axis=1)
        v_wide = jnp.concatenate([v, minus_one], axis=1)
        for start in range(0, slots, BLOCK):
            stop = start + BLOCK
            scores = lax.dot_general(
                k_wide[:stop], q_wide[start:stop], CONTRACT_LAST,
                preferred_element_type=jnp.float32,
            )
            last = jnp.where(later, MASKED, scores[start:stop])
            if start:
                scores = jnp.concatenate([scores[:start], last], axis=0)
            else:
                scores = last
            row_max = jnp.max(scores, axis=0, keepdims=True)
            exponent = jnp.exp2((scores - row_max) * (SCALE * LOG2_E))
            inverse = 1.0 / jnp.sum(exponent, axis=0, keepdims=True)
            grad_prob = lax.dot_general(
                v_wide[:stop], g_wide[start:stop], CONTRACT_LAST,
                preferred_element_type=jnp.float32,
            )
            grad_score = (exponent * (inverse * SCALE) * grad_prob).astype(jnp.bfloat16)
            prob_ref[:stop, start:stop] = (exponent * inverse).astype(jnp.bfloat16)
            score_ref[:stop, start:stop] = grad_score
        for start in range(0, slots, BLOCK):
            stop = start + BLOCK
            grad_query = jnp.dot(
                k_turned[:, :stop], score_ref[:stop, start:stop], preferred_element_type=jnp.float32
            ).T
            out_ref[start // CAP : stop // CAP, h * CAP : (h + 1) * CAP, 0:DH] = (
                grad_query.astype(jnp.bfloat16).reshape(BLOCK // CAP, CAP, DH)
            )
            for n, ref, other in ((1, score_ref, q), (2, prob_ref, g)):
                grad = jnp.dot(
                    ref[start:stop, start:], other[start:], preferred_element_type=jnp.float32
                )
                out_ref[
                    start // CAP : stop // CAP, h * CAP : (h + 1) * CAP, n * DH : (n + 1) * DH
                ] = grad.astype(jnp.bfloat16).reshape(BLOCK // CAP, CAP, DH)


def add_kernel(own_ref, *refs):
    *others, sum_ref, sent_ref = refs
    total = own_ref[...]
    for ref in others:
        total = total + ref[...].astype(jnp.float32)
    sum_ref[...] = total[0]
    sent_ref[...] = total.astype(jnp.bfloat16)


def unpack_kernel(home_ref, place_ref, dq_ref, dk_ref, dv_ref):
    owners = home_ref.shape[0]
    heads = home_ref.shape[1] // CAP
    slots = owners * CAP
    tokens = place_ref.shape[0]
    slot_iota = lax.broadcasted_iota(jnp.int32, (tokens, slots), 1)
    for h in range(heads):
        select = jnp.where(slot_iota == place_ref[:, h : h + 1], 1.0, 0.0).astype(jnp.bfloat16)
        rows = home_ref[:, h * CAP : (h + 1) * CAP, :].reshape(slots, 3 * DH)
        rows = jnp.dot(select, rows, preferred_element_type=jnp.float32).astype(jnp.bfloat16)
        for n, ref in enumerate((dq_ref, dk_ref, dv_ref)):
            ref[:, h * DH : (h + 1) * DH] = rows[:, n * DH : (n + 1) * DH]


def copies_to_all(block, axis):
    size = lax.axis_size(axis)
    return lax.all_to_all(
        jnp.broadcast_to(block[None], (size, *block.shape)), axis, 0, 0, tiled=True
    )


def forward(block, axis, shift):
    size = lax.axis_size(axis)
    return lax.ppermute(block, axis, [(i, (i + shift) % size) for i in range(size)])


def scatter_sum(blocks, axis):
    total = blocks[0]
    for n in range(1, lax.axis_size(axis)):
        total = total + forward(blocks[n].astype(jnp.bfloat16), axis, n).astype(jnp.float32)
    return total


def after(value, earlier):
    return lax.optimization_barrier((value, earlier))[0]


def local(
    query_rows, key_rows, value_rows, saved_output, output_grad, out_weight, cluster_id, _slot
):
    tokens, width = query_rows.shape
    heads = cluster_id.shape[0]
    owners = lax.axis_size(SEQ)
    bf16 = jnp.bfloat16
    shape = jax.ShapeDtypeStruct

    smem, vmem = (pl.BlockSpec(memory_space=space) for space in (pltpu.SMEM, pltpu.VMEM))
    here = jnp.stack([lax.axis_index(axis) for axis in (*SEQ, *HEAD)]).astype(jnp.int32)

    weight_z = copies_to_all(out_weight, Z).reshape(-1, width)
    qkv = pl.pallas_call(
        pack_kernel,
        out_shape=shape((owners, heads * CAP, 3 * DH), bf16),
        compiler_params=PARAMS,
        name="pack_rows",
    )(cluster_id, query_rows, key_rows, value_rows)
    pair = jnp.stack([output_grad, forward(output_grad, "core", 1)])
    qkv = lax.all_to_all(after(qkv, (weight_z[:16, :DH], pair)), SEQ, 0, 0, tiled=True)

    pairs = [pair] + [forward(pair, "y", n) for n in range(1, lax.axis_size("y"))]
    parts = [weight_z] + [forward(weight_z, "x", n) for n in range(1, lax.axis_size("x"))]
    cot, places = pl.pallas_call(
        cotangent_kernel,
        out_shape=(
            shape((owners * PAIR, DH), bf16),
            shape((tokens, 8), jnp.int32),
        ),
        in_specs=[smem] + [vmem] * (2 + len(parts) + len(pairs)),
        scratch_shapes=[pltpu.VMEM((len(parts), *weight_z.shape), bf16)],
        compiler_params=PARAMS,
        name="cotangent_rows",
    )(here, cluster_id, saved_output, *parts, *pairs)
    share = pl.pallas_call(
        share_kernel,
        out_shape=shape((4, 4, 4, out_weight.shape[0], width), jnp.float32),
        in_specs=[smem] + [vmem] * (1 + len(pairs)),
        compiler_params=PARAMS,
        name="weight_share",
    )(here, after(saved_output, places), *pairs)
    share = scatter_sum(share, "x")
    moved = [forward(share[n].astype(bf16), "z_lo", n) for n in range(1, 4)]
    cot, own, qkv = lax.optimization_barrier((cot, share[0], qkv))
    cot = cot.reshape(owners * PAIR // 2, 2, DH)
    cot = lax.all_to_all(cot, SEQ, 0, 0, tiled=True).reshape(owners * PAIR, DH)
    own, share = pl.pallas_call(
        add_kernel,
        out_shape=(shape(own.shape[1:], jnp.float32), shape(own.shape, bf16)),
        compiler_params=PARAMS,
        cost_estimate=EARLY,
        name="add_along_z_lo",
    )(own, *moved)
    moved = [forward(share[n], "z_hi", n) for n in range(1, 4)]
    grads = pl.pallas_call(
        attend_kernel,
        out_shape=shape((owners, heads * CAP, 3 * DH), bf16),
        scratch_shapes=[
            pltpu.VMEM((owners * CAP, owners * CAP), bf16),
            pltpu.VMEM((owners * CAP, owners * CAP), bf16),
        ],
        compiler_params=PARAMS,
        name="attend_cluster",
    )(qkv, cot)
    home = lax.all_to_all(grads, SEQ, 0, 0, tiled=True)
    dq, dk, dv = pl.pallas_call(
        unpack_kernel,
        out_shape=tuple(shape((tokens, width), bf16) for _ in range(3)),
        compiler_params=PARAMS,
        name="unpack_rows",
    )(home, places)
    own, moved, dq = lax.optimization_barrier((own, moved, dq))
    weight_grad = own + sum(block.astype(jnp.float32) for block in moved)
    return dq, dk, dv, weight_grad


def solution(mesh):
    n_head = mesh.devices.shape[1]
    grid = Mesh(mesh.devices.reshape(4, 4, 4, n_head // 2, 2), (*SEQ, *HEAD))
    rows, ids = P(SEQ, HEAD), P(HEAD, SEQ)
    return jax.shard_map(
        local,
        mesh=grid,
        in_specs=(rows,) * 6 + (ids,) * 2,
        out_specs=(rows,) * 4,
        check_vma=False,
    )
```

```python
import math

import jax
import jax.numpy as jnp
from jax import lax
from jax.experimental import pallas as pl
from jax.experimental.pallas import tpu as pltpu
from jax.sharding import Mesh
from jax.sharding import PartitionSpec as P

DH = 128
CAP = 16
PAIR = 2 * CAP + 2
BLOCK = 256
MASKED = -1e30
CONTRACT_LAST = (((1,), (1,)), ((), ()))
CONTRACT_FIRST = (((0,), (0,)), ((), ()))
SCALE = 1.0 / math.sqrt(DH)
LOG2_E = math.log2(math.e)
Z = ("z_hi", "z_lo")
SEQ = ("x", *Z)
HEAD = ("y", "core")
EARLY = pl.CostEstimate(flops=90_000_000_000, bytes_accessed=0, transcendentals=0)
PARAMS = pltpu.CompilerParams(vmem_limit_bytes=24 * 1024 * 1024)


def pair_places(ids, owners):
    heads, tokens = ids.shape
    earlier = (
        lax.broadcasted_iota(jnp.int32, (tokens, tokens), 0)
        < lax.broadcasted_iota(jnp.int32, (tokens, tokens), 1)
    ).astype(jnp.float32).astype(jnp.bfloat16)
    owner_iota = lax.broadcasted_iota(jnp.int32, (owners, tokens), 0)
    places = []
    for h in range(heads):
        onehot = jnp.where(owner_iota == ids[h : h + 1, :], 1.0, 0.0)
        before = jnp.dot(onehot.astype(jnp.bfloat16), earlier, preferred_element_type=jnp.float32)
        rank = jnp.sum(onehot * before, axis=0, keepdims=True)
        places.append((onehot, rank))
    return places


def pack_kernel(ids_ref, q_ref, k_ref, v_ref, out_ref):
    owners = out_ref.shape[0]
    ids = ids_ref[...]
    heads, tokens = ids.shape
    slots = owners * CAP
    slot_iota = lax.broadcasted_iota(jnp.int32, (slots, tokens), 0)
    for h, (_, rank) in enumerate(pair_places(ids, owners)):
        place = ids[h : h + 1, :] * CAP + rank.astype(jnp.int32)
        select = jnp.where(slot_iota == place, 1.0, 0.0).astype(jnp.bfloat16)
        columns = [ref[:, h * DH : (h + 1) * DH] for ref in (q_ref, k_ref, v_ref)]
        rows = jnp.dot(
            select, jnp.concatenate(columns, axis=1), preferred_element_type=jnp.float32
        )
        out_ref[:, h * CAP : (h + 1) * CAP, :] = rows.astype(jnp.bfloat16).reshape(
            owners, CAP, 3 * DH
        )


def block_of(here_ref, back, other):
    y = lax.rem(here_ref[3] + 4 - back, 4)
    return y, here_ref[4] + other - 2 * other * here_ref[4]


def share_kernel(here_ref, saved_ref, *refs):
    *pairs, out_ref = refs
    half = saved_ref.shape[1]
    depth = out_ref.shape[3]
    for back, pair in enumerate(pairs):
        for other in range(2):
            x, core = block_of(here_ref, back, other)
            share = lax.dot_general(
                pair[other], saved_ref[...], CONTRACT_FIRST, preferred_element_type=jnp.float32
            )
            for n in range(half // depth):
                ahead = [
                    lax.rem(there + 4 - here_ref[axis], 4)
                    for axis, there in ((0, x), (2, n % 4), (1, core * 2 + n // 4))
                ]
                out_ref[ahead[0], ahead[1], ahead[2]] = share[n * depth : (n + 1) * depth, :]


def cotangent_kernel(here_ref, ids_ref, saved_ref, *refs):
    *blocks, out_ref, place_ref, weight_ref = refs
    parts, pairs = blocks[:4], blocks[4:]
    sent = out_ref.shape[0]
    owners = sent // PAIR
    ids = ids_ref[...]
    heads, tokens = ids.shape
    width = saved_ref.shape[1]
    for back, part in enumerate(parts):
        weight_ref[lax.rem(here_ref[0] + 4 - back, 4)] = part[...]
    cot = jnp.zeros((tokens, width), jnp.float32)
    for back, pair in enumerate(pairs):
        for other in range(2):
            x, core = block_of(here_ref, back, other)
            rows = pl.ds(pl.multiple_of(core * width, width), width)
            cot = cot + jnp.dot(
                pair[other], weight_ref[x, rows, :], preferred_element_type=jnp.float32
            )
    cot = cot.astype(jnp.bfloat16)
    row_iota = lax.broadcasted_iota(jnp.int32, (sent, tokens), 0)
    lane = lax.broadcasted_iota(jnp.int32, (tokens, DH), 1)
    row8 = lax.broadcasted_iota(jnp.int32, (8, tokens), 0)
    meta = jnp.zeros((owners, DH), jnp.float32)
    message = jnp.zeros((sent, DH), jnp.float32)
    places = pair_places(ids, owners)
    rank_rows = jnp.zeros((8, tokens), jnp.float32)
    place_rows = jnp.zeros((8, tokens), jnp.float32)
    for h, (_, rank) in enumerate(places):
        place = ids[h : h + 1, :].astype(jnp.float32) * CAP + rank
        rank_rows = jnp.where(row8 == h, rank, rank_rows)
        place_rows = jnp.where(row8 == h, place, place_rows)
    rank_columns = rank_rows.T
    place_ref[...] = place_rows.T.astype(jnp.int32)
    for h, (onehot, rank) in enumerate(places):
        g = cot[:, h * DH : (h + 1) * DH]
        o = saved_ref[:, h * DH : (h + 1) * DH]
        row_term = jnp.sum(g.astype(jnp.float32) * o.astype(jnp.float32), axis=1, keepdims=True)
        row_term = row_term.astype(jnp.bfloat16).astype(jnp.float32)
        where_to = rank_columns[:, h : h + 1].astype(jnp.int32) + 2 * CAP * h
        spread = jnp.where(lane == where_to, row_term, 0.0) + jnp.where(
            lane == where_to + CAP, 1.0, 0.0
        )
        meta = meta + jnp.dot(
            onehot.astype(jnp.bfloat16),
            spread.astype(jnp.bfloat16),
            preferred_element_type=jnp.float32,
        )
        place = ids[h : h + 1, :] * PAIR + h * CAP + rank.astype(jnp.int32)
        select = jnp.where(row_iota == place, 1.0, 0.0).astype(jnp.bfloat16)
        message = message + jnp.dot(select, g, preferred_element_type=jnp.float32)
    meta_lane = lax.broadcasted_iota(jnp.int32, (owners, DH), 1)
    meta = jnp.where((meta_lane & CAP) != 0, (1.0 - meta) * MASKED, meta)
    meta_row = lax.broadcasted_iota(jnp.int32, (sent, owners), 1) * PAIR + heads * CAP
    select = lax.broadcasted_iota(jnp.int32, (sent, owners), 0) == meta_row
    message = message + jnp.dot(
        jnp.where(select, 1.0, 0.0).astype(jnp.bfloat16),
        meta.astype(jnp.bfloat16),
        preferred_element_type=jnp.float32,
    )
    out_ref[...] = message.astype(jnp.bfloat16)


def attend_kernel(qkv_ref, g_ref, out_ref, prob_ref, score_ref):
    owners = qkv_ref.shape[0]
    heads = qkv_ref.shape[1] // CAP
    slots = owners * CAP
    meta = jnp.concatenate(
        [
            jnp.broadcast_to(
                g_ref[first : first + 2, :].astype(jnp.float32)[:1], (CAP, DH)
            )
            for first in range(heads * CAP, owners * PAIR, PAIR)
        ],
        axis=0,
    )
    lane = lax.broadcasted_iota(jnp.int32, (slots, DH), 1)
    rank = lax.broadcasted_iota(jnp.int32, (slots, DH), 0) & (CAP - 1)
    later = lax.broadcasted_iota(jnp.int32, (BLOCK, BLOCK), 0) > lax.broadcasted_iota(
        jnp.int32, (BLOCK, BLOCK), 1
    )

    def rows_of(h, n):
        return qkv_ref[:, h * CAP : (h + 1) * CAP, n * DH : (n + 1) * DH].reshape(slots, DH)

    for h in range(heads):
        q, k, v = (rows_of(h, n) for n in range(3))
        g = jnp.concatenate(
            [g_ref[n : n + CAP, :] for n in range(h * CAP, owners * PAIR, PAIR)], axis=0
        )
        term_lanes = (lane >= 2 * CAP * h) & (lane < 2 * CAP * h + CAP)
        bias_lanes = (lane >= 2 * CAP * h + CAP) & (lane < 2 * CAP * (h + 1))
        own = jnp.where((lane & (CAP - 1)) == rank, meta, 0.0)
        extra = jnp.where(term_lanes | bias_lanes, own, 0.0).astype(jnp.bfloat16)
        minus_one = jnp.where(term_lanes, -1.0, 0.0).astype(jnp.bfloat16)
        one = jnp.where(bias_lanes, 1.0, 0.0).astype(jnp.bfloat16)
        k_turned = k.T
        q_wide = jnp.concatenate([q, one], axis=1)
        k_wide = jnp.concatenate([k, extra], axis=1)
        g_wide = jnp.concatenate([g, extra], axis=1)
        v_wide = jnp.concatenate([v, minus_one], axis=1)
        for start in range(0, slots, BLOCK):
            stop = start + BLOCK
            scores = lax.dot_general(
                k_wide[:stop], q_wide[start:stop], CONTRACT_LAST,
                preferred_element_type=jnp.float32,
            )
            last = jnp.where(later, MASKED, scores[start:stop])
            if start:
                scores = jnp.concatenate([scores[:start], last], axis=0)
            else:
                scores = last
            row_max = jnp.max(scores, axis=0, keepdims=True)
            exponent = jnp.exp2((scores - row_max) * (SCALE * LOG2_E))
            inverse = 1.0 / jnp.sum(exponent, axis=0, keepdims=True)
            grad_prob = lax.dot_general(
                v_wide[:stop], g_wide[start:stop], CONTRACT_LAST,
                preferred_element_type=jnp.float32,
            )
            grad_score = (exponent * (inverse * SCALE) * grad_prob).astype(jnp.bfloat16)
            prob_ref[:stop, start:stop] = (exponent * inverse).astype(jnp.bfloat16)
            score_ref[:stop, start:stop] = grad_score
        for start in range(0, slots, BLOCK):
            stop = start + BLOCK
            grad_query = jnp.dot(
                k_turned[:, :stop], score_ref[:stop, start:stop], preferred_element_type=jnp.float32
            ).T
            out_ref[start // CAP : stop // CAP, h * CAP : (h + 1) * CAP, 0:DH] = (
                grad_query.astype(jnp.bfloat16).reshape(BLOCK // CAP, CAP, DH)
            )
            for n, ref, other in ((1, score_ref, q), (2, prob_ref, g)):
                grad = jnp.dot(
                    ref[start:stop, start:], other[start:], preferred_element_type=jnp.float32
                )
                out_ref[
                    start // CAP : stop // CAP, h * CAP : (h + 1) * CAP, n * DH : (n + 1) * DH
                ] = grad.astype(jnp.bfloat16).reshape(BLOCK // CAP, CAP, DH)


def add_kernel(own_ref, *refs):
    *others, sum_ref, sent_ref = refs
    total = own_ref[...]
    for ref in others:
        total = total + ref[...].astype(jnp.float32)
    sum_ref[...] = total[0]
    sent_ref[...] = total.astype(jnp.bfloat16)


def unpack_kernel(home_ref, place_ref, dq_ref, dk_ref, dv_ref):
    owners = home_ref.shape[0]
    heads = home_ref.shape[1] // CAP
    slots = owners * CAP
    tokens = place_ref.shape[0]
    slot_iota = lax.broadcasted_iota(jnp.int32, (tokens, slots), 1)
    for h in range(heads):
        select = jnp.where(slot_iota == place_ref[:, h : h + 1], 1.0, 0.0).astype(jnp.bfloat16)
        rows = home_ref[:, h * CAP : (h + 1) * CAP, :].reshape(slots, 3 * DH)
        rows = jnp.dot(select, rows, preferred_element_type=jnp.float32).astype(jnp.bfloat16)
        for n, ref in enumerate((dq_ref, dk_ref, dv_ref)):
            ref[:, h * DH : (h + 1) * DH] = rows[:, n * DH : (n + 1) * DH]


def copies_to_all(block, axis):
    size = lax.axis_size(axis)
    return lax.all_to_all(
        jnp.broadcast_to(block[None], (size, *block.shape)), axis, 0, 0, tiled=True
    )


def forward(block, axis, shift):
    size = lax.axis_size(axis)
    return lax.ppermute(block, axis, [(i, (i + shift) % size) for i in range(size)])


def scatter_sum(blocks, axis):
    total = blocks[0]
    for n in range(1, lax.axis_size(axis)):
        total = total + forward(blocks[n].astype(jnp.bfloat16), axis, n).astype(jnp.float32)
    return total


def after(value, earlier):
    return lax.optimization_barrier((value, earlier))[0]


def local(
    query_rows, key_rows, value_rows, saved_output, output_grad, out_weight, cluster_id, _slot
):
    tokens, width = query_rows.shape
    heads = cluster_id.shape[0]
    owners = lax.axis_size(SEQ)
    bf16 = jnp.bfloat16
    shape = jax.ShapeDtypeStruct

    smem, vmem = (pl.BlockSpec(memory_space=space) for space in (pltpu.SMEM, pltpu.VMEM))
    here = jnp.stack([lax.axis_index(axis) for axis in (*SEQ, *HEAD)]).astype(jnp.int32)

    weight_z = copies_to_all(out_weight, Z).reshape(-1, width)
    qkv = pl.pallas_call(
        pack_kernel,
        out_shape=shape((owners, heads * CAP, 3 * DH), bf16),
        compiler_params=PARAMS,
        name="pack_rows",
    )(cluster_id, query_rows, key_rows, value_rows)
    pair = jnp.stack([output_grad, forward(output_grad, "core", 1)])
    qkv = lax.all_to_all(after(qkv, (weight_z[:16, :DH], pair)), SEQ, 0, 0, tiled=True)

    pairs = [pair] + [forward(pair, "y", n) for n in range(1, lax.axis_size("y"))]
    parts = [weight_z] + [forward(weight_z, "x", n) for n in range(1, lax.axis_size("x"))]
    cot, places = pl.pallas_call(
        cotangent_kernel,
        out_shape=(
            shape((owners * PAIR, DH), bf16),
            shape((tokens, 8), jnp.int32),
        ),
        in_specs=[smem] + [vmem] * (2 + len(parts) + len(pairs)),
        scratch_shapes=[pltpu.VMEM((len(parts), *weight_z.shape), bf16)],
        compiler_params=PARAMS,
        name="cotangent_rows",
    )(here, cluster_id, saved_output, *parts, *pairs)
    share = pl.pallas_call(
        share_kernel,
        out_shape=shape((4, 4, 4, out_weight.shape[0], width), jnp.float32),
        in_specs=[smem] + [vmem] * (1 + len(pairs)),
        compiler_params=PARAMS,
        name="weight_share",
    )(here, after(saved_output, places), *pairs)
    share = scatter_sum(share, "x")
    moved = [forward(share[n].astype(bf16), "z_lo", n) for n in range(1, 4)]
    cot, own, qkv = lax.optimization_barrier((cot, share[0], qkv))
    cot = cot.reshape(owners * PAIR // 2, 2, DH)
    cot = lax.all_to_all(cot, SEQ, 0, 0, tiled=True).reshape(owners * PAIR, DH)
    own, share = pl.pallas_call(
        add_kernel,
        out_shape=(shape(own.shape[1:], jnp.float32), shape(own.shape, bf16)),
        compiler_params=PARAMS,
        cost_estimate=EARLY,
        name="add_along_z_lo",
    )(own, *moved)
    moved = [forward(share[n], "z_hi", n) for n in range(1, 4)]
    grads = pl.pallas_call(
        attend_kernel,
        out_shape=shape((owners, heads * CAP, 3 * DH), bf16),
        scratch_shapes=[
            pltpu.VMEM((owners * CAP, owners * CAP), bf16),
            pltpu.VMEM((owners * CAP, owners * CAP), bf16),
        ],
        compiler_params=PARAMS,
        name="attend_cluster",
    )(qkv, cot)
    home = lax.all_to_all(grads, SEQ, 0, 0, tiled=True)
    dq, dk, dv = pl.pallas_call(
        unpack_kernel,
        out_shape=tuple(shape((tokens, width), bf16) for _ in range(3)),
        compiler_params=PARAMS,
        name="unpack_rows",
    )(home, places)
    own, moved, dq = lax.optimization_barrier((own, moved, dq))
    weight_grad = own + sum(block.astype(jnp.float32) for block in moved)
    return dq, dk, dv, weight_grad


def solution(mesh):
    n_head = mesh.devices.shape[1]
    grid = Mesh(mesh.devices.reshape(4, 4, 4, n_head // 2, 2), (*SEQ, *HEAD))
    rows, ids = P(SEQ, HEAD), P(HEAD, SEQ)
    return jax.shard_map(
        local,
        mesh=grid,
        in_specs=(rows,) * 6 + (ids,) * 2,
        out_specs=(rows,) * 4,
        check_vma=False,
    )
```
